256 devices in a mesh: vel: 16 (over z, core), space: 16 (over x, y).
Axes of the slice: x: 4, y: 4, z: 8, core: 2. Of those that a mesh axis runs over, the one named last changes fastest.
Arguments:
- particle_distribution: float32 [2048, 32, 2048], P('vel', None, 'space'), may hold values from 0 to 7, as said below
- piece_warmth: float32 [256], P('space'), may hold values from 0.6 to 1.8
- exterior_piece_label: int32 [2048], P('space'), may hold values from -1 to 255, as said below
Outputs:
- following_distribution: float32 [2048, 32, 2048], P('vel', None, 'space')
- revised_piece_warmth: float32 [256], P('space')
The draws below stay inside these ranges and needn't reach their ends.
Inputs may be any that keep to these rules, and one draw needn't show every extreme that they name: `particle_distribution`: every entry is positive. `exterior_piece_label`: one cyclic run of 512 consecutive columns holds the solid elements 0 to 255 in order, each on 2 consecutive columns; all other columns hold -1.
All inputs are finite; a program needn't handle non-finite values.
Results may differ from the reference program's by a relative error of at most 0.0003.
Values sent between devices are 32-bit elements; how exact they have to be, the bound alone decides.
A program may use at most 64 MiB of HBM per device.

```python
import math
import jax
import jax.numpy as jnp
from jax import lax

V = 2048
SPANWISE_CELLS = 32
LENGTHWISE_CELLS = 2048
TUBE_PIECES = 256


def draw_particle_distribution(key, part):
    key = jax.random.fold_in(key, 11)
    stochastic_seeds = jax.random.split(key, 6)
    indices = jnp.arange(V, dtype=jnp.int32)
    lengthwise_position = (((indices // 128).astype(jnp.float32) - 7.5) * 0.5)[:, None, None]
    circumferential_bearing = ((indices // 16 % 8).astype(jnp.float32) - 3.5)[:, None, None]
    spanwise_position = (((indices % 16).astype(jnp.float32) - 7.5) * 0.5)[:, None, None]
    lower_bound, upper_bound, coldest_value, hottest_value, convection_shift, jaggedness = (8.0, 32.0, 0.7, 1.4, 0.3, 0.4)
    particle_concentration = jnp.exp(jax.random.uniform(stochastic_seeds[0], (SPANWISE_CELLS, LENGTHWISE_CELLS), jnp.float32, math.log(lower_bound), math.log(upper_bound)))
    fluid_warmth = jax.random.uniform(stochastic_seeds[1], (SPANWISE_CELLS, LENGTHWISE_CELLS), jnp.float32, coldest_value, hottest_value)
    lengthwise_speed = jax.random.uniform(stochastic_seeds[2], (SPANWISE_CELLS, LENGTHWISE_CELLS), jnp.float32, -convection_shift, convection_shift)
    spanwise_speed = jax.random.uniform(stochastic_seeds[3], (SPANWISE_CELLS, LENGTHWISE_CELLS), jnp.float32, -convection_shift, convection_shift)
    circumferential_speed = jax.random.uniform(stochastic_seeds[4], (SPANWISE_CELLS, LENGTHWISE_CELLS), jnp.float32, -convection_shift, convection_shift)
    mixing_weight = jax.random.uniform(stochastic_seeds[5], (V, SPANWISE_CELLS, LENGTHWISE_CELLS), jnp.float32, 1.0 - jaggedness, 1.0 + jaggedness)
    warmth_spread = (lengthwise_position - lengthwise_speed) ** 2 + (spanwise_position - spanwise_speed) ** 2 + (circumferential_bearing - circumferential_speed) ** 2
    return particle_concentration * jnp.exp(-1.5 * jnp.log(2.0 * math.pi * fluid_warmth) - warmth_spread / (2.0 * fluid_warmth)) * mixing_weight


def draw_exterior_piece_label(key, part):
    key = jax.random.fold_in(key, 23)
    split_keys = jax.random.split(key, 3)
    several = jax.random.randint(split_keys[0], (8,), 0, LENGTHWISE_CELLS).astype(jnp.int32)
    shuffled = jax.random.permutation(split_keys[1], LENGTHWISE_CELLS).astype(jnp.int32)
    raw_bits = (jax.random.bits(split_keys[2], (4,)) % LENGTHWISE_CELLS).astype(jnp.int32)
    opening = (jnp.sum(several) + shuffled[0] + jnp.sum(raw_bits)) % LENGTHWISE_CELLS
    offset = (jnp.arange(LENGTHWISE_CELLS, dtype=jnp.int32) - opening) % LENGTHWISE_CELLS
    heated = LENGTHWISE_CELLS // 4
    return jnp.where(offset < heated, offset * TUBE_PIECES // heated, -1).astype(jnp.int32)


def steps_of(own_key, extent, pieces, low, top_value):
    factor_of, own = 1.0, jax.random.fold_in(own_key, 6)
    for axis_at, parts in pieces:
        steps = jnp.exp(jax.random.uniform(jax.random.fold_in(own, axis_at), (parts,), jnp.float32, low / len(pieces), top_value / len(pieces)))
        factor_of = factor_of * jnp.repeat(steps, extent[axis_at] // parts).reshape([-1 if axis == axis_at else 1 for axis in range(len(extent))])
    return factor_of


def setup_inputs(seed: int = 0) -> dict:
    arg_keys = jax.random.split(jax.random.key(seed), 4)
    return {
        "particle_distribution": draw_particle_distribution(jax.random.fold_in(arg_keys[3], 71), 0),
        "piece_warmth": jnp.clip(0.6 + 1.1999999 * jax.random.uniform(arg_keys[1], (TUBE_PIECES,), jnp.float32) ** steps_of(arg_keys[1], (TUBE_PIECES,), ((0, 16),), -0.2, 0.2), 0.6, 1.8),
        "exterior_piece_label": draw_exterior_piece_label(jax.random.fold_in(arg_keys[3], 71), 0),
    }


STEP_DURATION = 0.25
HALF_STEP = 0.125
COLLISION_SPAN = 8.0
WEIGHT = 0.25
TUBE_TRANSFER = 0.45
CONDUCTION_LINK = 0.1
CEILING_TIER = lax.Precision.HIGHEST


def speeds(offset, number):
    indices = offset + jnp.arange(number, dtype=jnp.int32)
    lengthwise_position = ((indices // 128).astype(jnp.float32) - 7.5) * 0.5
    circumferential_bearing = ((indices // 16) % 8).astype(jnp.float32) - 3.5
    spanwise_position = ((indices % 16).astype(jnp.float32) - 7.5) * 0.5
    return lengthwise_position, spanwise_position, circumferential_bearing


def moment_table(lengthwise_position, spanwise_position, circumferential_bearing):
    internal_enthalpy = 0.5 * (lengthwise_position * lengthwise_position + spanwise_position * spanwise_position + circumferential_bearing * circumferential_bearing)
    return WEIGHT * jnp.stack([jnp.ones_like(lengthwise_position), lengthwise_position, spanwise_position, circumferential_bearing, internal_enthalpy])


def wall_table(lengthwise_position, spanwise_position, circumferential_bearing):
    internal_enthalpy = 0.5 * (lengthwise_position * lengthwise_position + spanwise_position * spanwise_position + circumferential_bearing * circumferential_bearing)
    upward = spanwise_position > 0.0
    inward = jnp.where(upward, spanwise_position, 0.0)
    outward = jnp.where(upward, 0.0, -spanwise_position)
    return WEIGHT * jnp.stack([inward, inward * internal_enthalpy, outward, outward * internal_enthalpy])


def moments(moment_rows, values):
    flattened = values.reshape(values.shape[0], -1)
    summed = jnp.dot(moment_rows, flattened, precision=CEILING_TIER)
    return summed.reshape((moment_rows.shape[0],) + values.shape[1:])


def gas_state(quadrature_totals):
    particle_concentration = quadrature_totals[0]
    lengthwise_speed = quadrature_totals[1] / particle_concentration
    spanwise_speed = quadrature_totals[2] / particle_concentration
    circumferential_speed = quadrature_totals[3] / particle_concentration
    fluid_warmth = (2.0 * quadrature_totals[4] / particle_concentration - (lengthwise_speed * lengthwise_speed + spanwise_speed * spanwise_speed + circumferential_speed * circumferential_speed)) / 3.0
    collision_frequency = COLLISION_SPAN * jnp.exp(-0.19 * jnp.log(fluid_warmth)) / particle_concentration
    return jnp.stack([particle_concentration, lengthwise_speed, spanwise_speed, circumferential_speed, fluid_warmth, collision_frequency])


def maxwell(lengthwise_position, spanwise_position, circumferential_bearing, hydrodynamic_fields):
    warmth_spread = (lengthwise_position - hydrodynamic_fields[1]) ** 2 + (spanwise_position - hydrodynamic_fields[2]) ** 2 + (circumferential_bearing - hydrodynamic_fields[3]) ** 2
    return hydrodynamic_fields[0] * jnp.exp(-1.5 * jnp.log(2.0 * math.pi * hydrodynamic_fields[4]) - warmth_spread / (2.0 * hydrodynamic_fields[4]))


def half_step(values, hydrodynamic_fields, lengthwise_position, spanwise_position, circumferential_bearing):
    doubled = 2.0 * hydrodynamic_fields[5]
    target = maxwell(lengthwise_position, spanwise_position, circumferential_bearing, hydrodynamic_fields)
    return (doubled - HALF_STEP) / (doubled + STEP_DURATION) * values + 3.0 * HALF_STEP / (doubled + STEP_DURATION) * target


def face_mix(values, hydrodynamic_fields, lengthwise_position, spanwise_position, circumferential_bearing):
    doubled = 2.0 * hydrodynamic_fields[5]
    target = maxwell(lengthwise_position, spanwise_position, circumferential_bearing, hydrodynamic_fields)
    return doubled / (doubled + HALF_STEP) * values + HALF_STEP / (doubled + HALF_STEP) * target


def minmod(forward, backward):
    return 0.5 * (jnp.sign(forward) + jnp.sign(backward)) * jnp.minimum(jnp.abs(forward), jnp.abs(backward))


def upwind_faces(widened, velocity, dimension):
    number = widened.shape[dimension] - 4
    steps_along = lax.slice_in_dim(widened, 1, number + 4, axis=dimension) - lax.slice_in_dim(widened, 0, number + 3, axis=dimension)
    slopes = minmod(lax.slice_in_dim(steps_along, 1, number + 3, axis=dimension), lax.slice_in_dim(steps_along, 0, number + 2, axis=dimension))
    upper = lax.slice_in_dim(widened, 1, number + 2, axis=dimension) + (0.5 - velocity * HALF_STEP) * lax.slice_in_dim(slopes, 0, number + 1, axis=dimension)
    lower = lax.slice_in_dim(widened, 2, number + 3, axis=dimension) + (-0.5 - velocity * HALF_STEP) * lax.slice_in_dim(slopes, 1, number + 2, axis=dimension)
    return jnp.where(velocity > 0.0, upper, lower)


def mirror(values):
    number = values.shape[0]
    folded = values.reshape((number // 16, 16) + values.shape[1:])
    return jnp.flip(folded, 1).reshape(values.shape)


def with_ghosts(values):
    flipped = mirror(values)
    return jnp.concatenate([flipped[:, 1:2], flipped[:, 0:1], values, flipped[:, -1:], flipped[:, -2:-1]], axis=1)


def boundary_maxwellian_field(lengthwise_position, spanwise_position, circumferential_bearing, interface_warmth):
    internal_enthalpy = 0.5 * (lengthwise_position * lengthwise_position + spanwise_position * spanwise_position + circumferential_bearing * circumferential_bearing)
    return jnp.exp(-1.5 * jnp.log(2.0 * math.pi * interface_warmth) - internal_enthalpy / interface_warmth)


def wall_heat(wall_sums, strip_touches_tube):
    wall_density = wall_sums[0] / wall_sums[2]
    return jnp.where(strip_touches_tube, wall_sums[1] - wall_density * wall_sums[3], 0.0)


def wall_faces(flux_radial, outer_values, wall_sums, boundary_maxwellian, strip_touches_tube, radial_column):
    wall_density = wall_sums[0] / wall_sums[2]
    reflected = jnp.where(radial_column > 0.0, outer_values, wall_density * boundary_maxwellian)
    outer_face = jnp.where(strip_touches_tube, reflected, flux_radial[:, -1])
    return jnp.concatenate([flux_radial[:, :-1], outer_face[:, None]], axis=1)


def advance(values, plus_half, flux_axial, flux_radial, lengthwise_position, spanwise_position):
    return 4.0 / 3.0 * plus_half - values / 3.0 - STEP_DURATION * (lengthwise_position * (flux_axial[:, :, 1:] - flux_axial[:, :, :-1]) + spanwise_position * (flux_radial[:, 1:] - flux_radial[:, :-1]))


def reference(particle_distribution, piece_warmth, exterior_piece_label):
    grouped = particle_distribution.reshape(V // 128, 128, SPANWISE_CELLS, LENGTHWISE_CELLS)
    offsets = jnp.arange(V // 128, dtype=jnp.int32) * 128

    def cell_sum(running, element):
        block, offset = element
        lengthwise_position, spanwise_position, circumferential_bearing = speeds(offset, 128)
        return running + moments(moment_table(lengthwise_position, spanwise_position, circumferential_bearing), block), None

    cell_sums, unused = lax.scan(cell_sum, jnp.zeros((5, SPANWISE_CELLS, LENGTHWISE_CELLS), jnp.float32), (grouped, offsets))
    macro_cells = gas_state(cell_sums)
    strip_touches_tube = exterior_piece_label >= 0
    piece_label = jnp.arange(TUBE_PIECES, dtype=jnp.int32)
    piece_marker = (exterior_piece_label[None, :] == piece_label[:, None]).astype(jnp.float32)
    interface_warmth = jnp.where(strip_touches_tube, jnp.dot(piece_warmth, piece_marker, precision=CEILING_TIER), 1.0)

    def local_faces(block, offset):
        lengthwise_position, spanwise_position, circumferential_bearing = speeds(offset, 128)
        plus_half = half_step(block, macro_cells, lengthwise_position[:, None, None], spanwise_position[:, None, None], circumferential_bearing[:, None, None])
        widened = jnp.concatenate([plus_half[:, :, -2:], plus_half, plus_half[:, :, :2]], axis=2)
        values_axial = upwind_faces(widened, lengthwise_position[:, None, None], 2)
        values_radial = upwind_faces(with_ghosts(plus_half), spanwise_position[:, None, None], 1)
        boundary_maxwellian = boundary_maxwellian_field(lengthwise_position[:, None], spanwise_position[:, None], circumferential_bearing[:, None], interface_warmth)
        return plus_half, values_axial, values_radial, boundary_maxwellian

    def face_sum(running, element):
        block, offset = element
        lengthwise_position, spanwise_position, circumferential_bearing = speeds(offset, 128)
        plus_half, values_axial, values_radial, boundary_maxwellian = local_faces(block, offset)
        moment_rows = moment_table(lengthwise_position, spanwise_position, circumferential_bearing)
        wall_weights = wall_table(lengthwise_position, spanwise_position, circumferential_bearing)
        wall_part = jnp.concatenate([jnp.dot(wall_weights[0:2], values_radial[:, -1], precision=CEILING_TIER), jnp.dot(wall_weights[2:4], boundary_maxwellian, precision=CEILING_TIER)])
        return (running[0] + moments(moment_rows, values_axial), running[1] + moments(moment_rows, values_radial), running[2] + wall_part), None

    start_sums = (jnp.zeros((5, SPANWISE_CELLS, LENGTHWISE_CELLS + 1), jnp.float32), jnp.zeros((5, SPANWISE_CELLS + 1, LENGTHWISE_CELLS), jnp.float32), jnp.zeros((4, LENGTHWISE_CELLS), jnp.float32))
    face_sums, unused = lax.scan(face_sum, start_sums, (grouped, offsets))
    macro_axial = gas_state(face_sums[0])
    macro_radial = gas_state(face_sums[1])
    wall_sums = face_sums[2]
    heat_flow = wall_heat(wall_sums, strip_touches_tube)

    def update(element):
        block, offset = element
        lengthwise_position, spanwise_position, circumferential_bearing = speeds(offset, 128)
        plus_half, values_axial, values_radial, boundary_maxwellian = local_faces(block, offset)
        axial_grid = lengthwise_position[:, None, None]
        radial_grid = spanwise_position[:, None, None]
        azimuth_grid = circumferential_bearing[:, None, None]
        flux_axial = face_mix(values_axial, macro_axial, axial_grid, radial_grid, azimuth_grid)
        flux_radial = face_mix(values_radial, macro_radial, axial_grid, radial_grid, azimuth_grid)
        flux_radial = wall_faces(flux_radial, values_radial[:, -1], wall_sums, boundary_maxwellian, strip_touches_tube, spanwise_position[:, None])
        return advance(block, plus_half, flux_axial, flux_radial, axial_grid, radial_grid)

    following_distribution = lax.map(update, (grouped, offsets)).reshape(V, SPANWISE_CELLS, LENGTHWISE_CELLS)
    warmth_received = jnp.dot(piece_marker, heat_flow, precision=CEILING_TIER)
    condition_spread = piece_warmth - 1.0
    ghost_margin = jnp.pad(condition_spread, 1)
    revised_piece_warmth = piece_warmth + TUBE_TRANSFER * (ghost_margin[:-2] - 2.0 * condition_spread + ghost_margin[2:]) + CONDUCTION_LINK * STEP_DURATION * warmth_received
    return following_distribution, revised_piece_warmth
```

```python
import functools
import math

import jax
import jax.numpy as jnp
from jax import lax
from jax.experimental import pallas as pl
from jax.experimental.pallas import tpu as pltpu
from jax.sharding import PartitionSpec as P

MESH = pl.DeviceIdType.MESH
N = 16
ROWS = 32
LANES = 128
TWO_PI = 2.0 * math.pi
BITREV = (0, 4, 2, 6, 1, 5, 3, 7)
F32 = jnp.float32


def iota(axis):
    return lax.broadcasted_iota(jnp.int32, (8, LANES), axis)


def spread(row):
    return jnp.broadcast_to(row, (8, LANES))


def minmod(p, q):
    return jnp.maximum(jnp.minimum(p, 0.0), jnp.minimum(jnp.maximum(p, 0.0), q))


def flip8(x, sub):
    x = pltpu.roll(x, 4, 0)
    x = jnp.where((sub & 2) == 0, pltpu.roll(x, 6, 0), pltpu.roll(x, 2, 0))
    return jnp.where((sub & 1) == 0, pltpu.roll(x, 7, 0), pltpu.roll(x, 1, 0))


def merge(a, b, h, sub):
    low = (sub & h) == 0
    if h == 4:
        return jnp.where(low, a, b) + pltpu.roll(jnp.where(low, b, a), 4, 0)
    return jnp.where(low, a, pltpu.roll(b, h, 0)) + jnp.where(
        low, pltpu.roll(a, 8 - h, 0), b
    )


def stack_sums(parts, sub):
    x = [parts[BITREV[i]] for i in range(8)]
    x = [merge(x[2 * i], x[2 * i + 1], 4, sub) for i in range(4)]
    x = [merge(x[2 * i], x[2 * i + 1], 2, sub) for i in range(2)]
    return merge(x[0], x[1], 1, sub)


def z_sums(v):
    s = [v[4 + j] + v[3 - j] for j in range(4)]
    d = [v[4 + j] - v[3 - j] for j in range(4)]
    total = (s[0] + s[1]) + (s[2] + s[3])
    first = (0.5 * d[0] + 1.5 * d[1]) + (2.5 * d[2] + 3.5 * d[3])
    second = (0.25 * s[0] + 2.25 * s[1]) + (6.25 * s[2] + 12.25 * s[3])
    return total, first, second


def quads(low, high, y):
    s0, z0, zz0 = z_sums(low)
    s1, z1, zz1 = z_sums(high)
    a0, a1 = y[0] * s0, y[1] * s1
    return (s0 + s1, a0 + a1, z0 + z1, (y[0] * a0 + y[1] * a1) + (zz0 + zz1)), (
        a1,
        y[1] * (y[1] * a1 + zz1),
    )


def gas(total, by_x, by_xx, sub, face):
    s0 = total
    ux = by_x / s0
    uy = pltpu.roll(total, 6, 0) / s0
    uz = pltpu.roll(total, 4, 0) / s0
    rho = 0.25 * s0
    temp = ((by_xx + pltpu.roll(total, 2, 0)) / s0 - (ux * ux + uy * uy + uz * uz)) / 3.0
    tau = 8.0 * jnp.exp(-0.19 * jnp.log(temp)) / rho
    if face:
        mix = 2.0 * tau / (2.0 * tau + 0.125)
        share = 0.125 / (2.0 * tau + 0.125)
    else:
        mix = (2.0 * tau - 0.125) / (2.0 * tau + 0.25)
        share = 0.375 / (2.0 * tau + 0.25)
    weight = share * rho * jnp.exp(-1.5 * jnp.log(TWO_PI * temp))
    half = 0.5 / temp
    first = jnp.where(
        sub < 2,
        mix,
        jnp.where(
            sub < 4,
            pltpu.roll(weight, 2, 0),
            jnp.where(sub < 6, pltpu.roll(ux, 4, 0), pltpu.roll(uy, 6, 0)),
        ),
    )
    second = jnp.where(sub < 2, uz, pltpu.roll(half, 2, 0))
    return first, second


def gather_sums(ref):
    total = by_x = by_xx = None
    for k in range(N):
        x = 0.5 * (k - 7.5)
        t = ref[k]
        if k == 0:
            total, by_x, by_xx = t, x * t, (x * x) * t
        else:
            total, by_x, by_xx = total + t, by_x + x * t, by_xx + (x * x) * t
    return total, by_x, by_xx


def kernel(
    f_hbm, pw_ref, lab_ref, out_hbm, rev_ref,
    fv, plus, gx, gy,
    s1, r1, a1, sx, rx, ax_f, sy, ry, ay_f, s32, r32, sex, rex,
    warm, heat, pk, pku, pkd, cpk, gpk, prev, x8_ref, fx_ref, fp_ref,
    in_sem, out_sem, send, recv, hsend, hrecv,
):
    me = lax.axis_index("vel")
    sp = lax.axis_index("space")
    ip = (me >= 8).astype(jnp.int32)
    dirn = 2 * ip - 1
    xi_x = 0.5 * (me.astype(F32) - 7.5)
    abs_x = xi_x * dirn.astype(F32)
    sub, lane = iota(0), iota(1)
    subf = sub.astype(F32)
    y = (0.5 * (subf - 7.5), 0.5 * (subf + 0.5))
    zed = subf - 3.5
    step_dn = lax.rem(dirn + 128, 128)
    step_up = lax.rem(128 - dirn, 128)
    at_up = lane == 127 - 127 * ip
    at_dn = lane == 127 * ip
    is_pos = lane < 128 * ip

    def vel_copy(group, d, src, dst):
        peer = lax.rem(me + d, N)
        return pltpu.make_async_remote_copy(
            src, dst, send.at[group, d], recv.at[group, d],
            device_id={"vel": peer}, device_id_type=MESH,
        )

    def space_copy(group, d, src, dst):
        peer = lax.rem(sp + d, N)
        return pltpu.make_async_remote_copy(
            src, dst, hsend.at[group, d], hrecv.at[group, d],
            device_id={"space": peer}, device_id_type=MESH,
        )

    def wait_all(copier, group, buf, mine, ready=True):
        @pl.loop(1, N)
        def _(d):
            src = lax.rem(mine - d + N, N)
            c = copier(group, d, buf.at[src], buf.at[src])
            if ready:
                c.wait_recv()
            else:
                c.wait_send()

    @pl.loop(0, ROWS)
    def _(r):
        pltpu.make_async_copy(f_hbm.at[:, r], fv.at[r], in_sem.at[r]).start()

    barrier = pltpu.get_barrier_semaphore()

    @pl.loop(1, N)
    def _(d):
        pl.semaphore_signal(
            barrier, 1, device_id={"vel": lax.rem(me + d, N)}, device_id_type=MESH
        )
        pl.semaphore_signal(
            barrier, 1, device_id={"space": lax.rem(sp + d, N)}, device_id_type=MESH
        )

    own = jnp.broadcast_to(pw_ref[...], (16, 16))
    diag = lax.broadcasted_iota(jnp.int32, (16, 16), 0) == lax.broadcasted_iota(
        jnp.int32, (16, 16), 1
    )
    own = jnp.sum(jnp.where(diag, own, 0.0), axis=1, keepdims=True)
    warm[sp] = jnp.broadcast_to(own, (16, LANES))
    zero = jnp.zeros((8, LANES), F32)
    for i in range(16):
        pk[i] = zero

    def load16(ref, r):
        return [
            [ref[r, pl.ds(iz * 16 + half * 8, 8), :] for iz in range(8)] for half in range(2)
        ]

    @pl.loop(0, N)
    def _(o):
        parts = [None] * 8
        for row in range(2):
            r = 2 * o + row
            pltpu.make_async_copy(f_hbm.at[:, r], fv.at[r], in_sem.at[r]).wait()
            v = load16(fv, r)
            q, _w = quads(v[0], v[1], y)
            for i in range(4):
                parts[2 * i + row] = q[i]
        s1[o] = stack_sums(parts, sub)

    r1[me] = s1[me]
    pl.semaphore_wait(barrier, 2 * (N - 1))

    @pl.loop(1, N)
    def _(d):
        peer = lax.rem(me + d, N)
        vel_copy(0, d, s1.at[peer], r1.at[me]).start()

    @pl.loop(1, N)
    def _(d):
        space_copy(0, d, warm.at[sp], warm.at[sp]).start()

    wait_all(vel_copy, 0, r1, me)
    first, second = gas(*gather_sums(r1), sub, False)
    a1[me, 0:8, :] = first
    a1[me, 8:16, :] = second

    @pl.loop(1, N)
    def _(d):
        vel_copy(1, d, a1.at[me], a1.at[me]).start()

    wait_all(space_copy, 0, warm, sp)
    label = spread(lab_ref[...])
    walled = label >= 0
    tw_sum = zero
    for k in range(N):
        for h in range(2):
            tw_sum = tw_sum + jnp.where(
                label == k * 16 + h * 8 + sub, warm[k, pl.ds(8 * h, 8), :], 0.0
            )
    tw_sum = spread(jnp.sum(tw_sum, axis=0, keepdims=True))
    tw = jnp.where(walled, tw_sum, 1.0)
    half_tw = 0.5 / tw
    wall_norm = jnp.exp(-1.5 * jnp.log(TWO_PI * tw))
    e_xy = jnp.exp(-(y[1] * y[1]) * half_tw)
    e_z = jnp.exp(-(zed * zed) * half_tw)

    def down(t):
        return spread(jnp.sum(t, axis=0, keepdims=True))

    sum_x, sum_xx = 2.0 * down(e_xy), 2.0 * down(y[1] * y[1] * e_xy)
    sum_z, sum_zz = down(e_z), down(zed * zed * e_z)
    sum_y1, sum_y3 = down(y[1] * e_xy), down(y[1] * y[1] * y[1] * e_xy)
    out_mass = wall_norm * (sum_x * sum_z * sum_y1)
    out_energy = 0.5 * wall_norm * (
        sum_xx * sum_z * sum_y1 + sum_x * sum_zz * sum_y1 + sum_x * sum_z * sum_y3
    )

    wait_all(vel_copy, 1, a1, me)

    def factors(first, second, row):
        mix = spread(first[0 + row : 1 + row])
        weight = spread(first[2 + row : 3 + row])
        ux = spread(first[4 + row : 5 + row])
        uy = spread(first[6 + row : 7 + row])
        uz = spread(second[0 + row : 1 + row])
        half = spread(second[2 + row : 3 + row])
        ey = [jnp.exp(-((y[h] - uy) * (y[h] - uy)) * half) for h in range(2)]
        dz, dx = zed - uz, xi_x - ux
        bz = weight * jnp.exp(-(dz * dz + dx * dx) * half)
        return mix, ey, bz

    @pl.loop(0, N)
    def _(o):
        first, second = a1[o, 0:8, :], a1[o, 8:16, :]
        for row in range(2):
            r = 2 * o + row
            mix, ey, bz = factors(first, second, row)
            shift = 4 * r + 1 + ip
            mask = (lane >= 4 * r) & (lane <= 4 * r + 2)
            for iz in range(8):
                b = spread(bz[iz : iz + 1])
                for h in range(2):
                    at = pl.ds(iz * 16 + h * 8, 8)
                    p = mix * fv[r, at, :] + ey[h] * b
                    plus[r + 2, at, :] = p
                    i = iz * 2 + h
                    pk[i] = jnp.where(mask, pltpu.roll(p, shift, 1), pk[i])

    down_d = lax.rem(dirn + N, N)
    up_d = lax.rem(N - dirn, N)
    to_down = pltpu.make_async_remote_copy(
        pk, pku, hsend.at[2, 0], hrecv.at[2, 0],
        device_id={"space": lax.rem(sp + down_d, N)}, device_id_type=MESH,
    )
    to_up = pltpu.make_async_remote_copy(
        pk, pkd, hsend.at[2, 1], hrecv.at[2, 1],
        device_id={"space": lax.rem(sp + up_d, N)}, device_id_type=MESH,
    )
    to_down.start()
    to_up.start()

    for ghost, real in ((1, 2), (0, 3), (34, 33), (35, 32)):
        @pl.loop(0, 8)
        def _(iz):
            lo = pl.multiple_of(iz * 16, 8)
            hi = pl.multiple_of(iz * 16 + 8, 8)
            x0, x1 = plus[real, pl.ds(lo, 8), :], plus[real, pl.ds(hi, 8), :]
            plus[ghost, pl.ds(lo, 8), :] = flip8(x1, sub)
            plus[ghost, pl.ds(hi, 8), :] = flip8(x0, sub)

    cy = (0.5 + 0.125 * y[0], 0.5 - 0.125 * y[1])

    def y_face(j):
        v = [[None] * 8, [None] * 8]
        for iz in range(8):
            for h in range(2):
                at = pl.ds(iz * 16 + h * 8, 8)
                if h:
                    c, b, a = plus[j + 1, at, :], plus[j, at, :], plus[j + 2, at, :]
                else:
                    c, b, a = plus[j + 2, at, :], plus[j + 3, at, :], plus[j + 1, at, :]
                g = c + cy[h] * minmod(a - c, c - b)
                gy[j, at, :] = g
                v[h][iz] = g
        return quads(v[0], v[1], y)

    def ship(group, o, src, dst_own, dst):
        d = lax.rem(o - me + N, N)

        @pl.when(d != 0)
        def _():
            vel_copy(group, d, src.at[o], dst.at[me]).start()

    q, w = y_face(32)
    s32[...] = stack_sums([q[0], w[0], q[1], w[1], q[2], zero, q[3], zero], sub)
    r32[me] = s32[...]

    @pl.loop(1, N)
    def _(d):
        vel_copy(2, d, s32, r32.at[me]).start()

    @pl.loop(0, N)
    def _(i):
        o = lax.rem(me + 8 + i, N)
        parts = [None] * 8
        for row in range(2):
            q, _w = y_face(2 * o + row)
            for k in range(4):
                parts[2 * k + row] = q[k]
        sy[o] = stack_sums(parts, sub)
        ship(3, o, sy, None, ry)

    ry[me] = sy[me]

    to_down.wait_recv()
    to_up.wait_recv()
    cx = 0.5 - 0.125 * abs_x
    centre = (lane & 3) == 1
    v = [[None] * 8, [None] * 8]
    for iz in range(8):
        for h in range(2):
            i = iz * 2 + h
            u = pku[i]
            own_pk = pk[i]
            u2 = pltpu.roll(u, step_dn, 1)
            w0 = pltpu.roll(own_pk, step_up, 1)
            d_o = pltpu.roll(pkd[i], step_up, 1)
            g = u + cx * minmod(w0 - u, u - u2)
            gpk[i] = g
            v[h][iz] = g
            cpk[i] = jnp.where(centre, u, pltpu.roll(d_o - own_pk, step_up, 1))
    q, _w = quads(v[0], v[1], y)
    parts = [None] * 8
    for k in range(4):
        parts[2 * k] = q[k]
        parts[2 * k + 1] = pltpu.roll(q[k], 124, 1)
    x8 = stack_sums(parts, sub)
    x8_ref[...] = x8
    sex[...] = jnp.where(is_pos, 0.0, x8)

    @pl.loop(0, N)
    def _(i):
        o = lax.rem(me + 8 + i, N)
        parts = [None] * 8
        for row in range(2):
            r = 2 * o + row
            shift = 126 - 4 * r + ip
            v = [[None] * 8, [None] * 8]
            for iz in range(8):
                for h in range(2):
                    at = pl.ds(iz * 16 + h * 8, 8)
                    p = plus[r + 2, at, :]
                    edge = pltpu.roll(cpk[iz * 2 + h], shift, 1)
                    e = p - jnp.where(at_up, edge, pltpu.roll(p, step_dn, 1))
                    en = jnp.where(at_dn, edge, pltpu.roll(e, step_up, 1))
                    g = p + cx * minmod(en, e)
                    gx[r, at, :] = g
                    v[h][iz] = g
            q, _w = quads(v[0], v[1], y)
            for k in range(4):
                parts[2 * k + row] = q[k]
        t = stack_sums(parts, sub)
        at_o = (lane == 8 * o + 1) & is_pos
        sex[...] = jnp.where(at_o, pltpu.roll(t, 8 * o + 2, 1), sex[...])
        sx[o] = jnp.where(
            lane < ip, pltpu.roll(x8_ref[...], 127 - 8 * o, 1), pltpu.roll(t, ip, 1)
        )
        ship(4, o, sx, None, rx)

    rx[me] = sx[me]
    rex[me] = sex[...]

    @pl.loop(1, N)
    def _(d):
        vel_copy(5, d, sex, rex.at[me]).start()

    @pl.loop(0, ROWS)
    def _(r):
        for i in range(16):
            at = pl.ds(i * 8, 8)
            fv[r, at, :] = (4.0 / 3.0) * plus[r + 2, at, :] - fv[r, at, :] * (1.0 / 3.0)

    wait_all(vel_copy, 3, ry, me)
    first, second = gas(*gather_sums(ry), sub, True)
    ay_f[me, 0:8, :] = first
    ay_f[me, 8:16, :] = second

    @pl.loop(1, N)
    def _(d):
        vel_copy(6, d, ay_f.at[me], ay_f.at[me]).start()

    wait_all(vel_copy, 4, rx, me)
    first, second = gas(*gather_sums(rx), sub, True)
    ax_f[me, 0:8, :] = first
    ax_f[me, 8:16, :] = second

    @pl.loop(1, N)
    def _(d):
        vel_copy(7, d, ax_f.at[me], ax_f.at[me]).start()

    wait_all(vel_copy, 2, r32, me)
    total, by_x, by_xx = gather_sums(r32)
    wall_first, wall_second = gas(total, by_x, by_xx, sub, True)
    in_mass = spread(total[1:2])
    in_energy = 0.5 * spread(by_xx[1:2] + total[3:4])
    rho_w = in_mass / out_mass
    flow = jnp.where(walled, 0.25 * (in_energy - rho_w * out_energy), 0.0)
    heat[sp] = jnp.where(sub == 0, flow, label.astype(F32))

    @pl.loop(1, N)
    def _(d):
        space_copy(1, d, heat.at[sp], heat.at[sp]).start()

    wait_all(vel_copy, 5, rex, me)
    fx_first, fx_second = gas(*gather_sums(rex), sub, True)
    fx_ref[0:8, :] = fx_first
    fx_ref[8:16, :] = fx_second

    wait_all(vel_copy, 6, ay_f, me)
    quarter_y = (0.25 * y[0], 0.25 * y[1])

    def y_flux(first, second, row, j):
        mix, ey, bz = factors(first, second, row)
        mix2 = [mix * quarter_y[h] for h in range(2)]
        ey2 = [ey[h] * quarter_y[h] for h in range(2)]
        out = []
        for iz in range(8):
            b = spread(bz[iz : iz + 1])
            for h in range(2):
                at = pl.ds(iz * 16 + h * 8, 8)
                out.append(mix2[h] * gy[j, at, :] + ey2[h] * b)
        return out

    def y_update(r, flux):
        for i in range(16):
            at = pl.ds(i * 8, 8)
            fv[r, at, :] = fv[r, at, :] - (flux[i] - prev[i])
            prev[i] = flux[i]

    flux = y_flux(ay_f[0, 0:8, :], ay_f[0, 8:16, :], 0, 0)
    for i in range(16):
        prev[i] = flux[i]

    @pl.loop(0, N - 1)
    def _(o):
        y_update(2 * o, y_flux(ay_f[o, 0:8, :], ay_f[o, 8:16, :], 1, 2 * o + 1))
        y_update(
            2 * o + 1, y_flux(ay_f[o + 1, 0:8, :], ay_f[o + 1, 8:16, :], 0, 2 * o + 2)
        )

    y_update(30, y_flux(ay_f[N - 1, 0:8, :], ay_f[N - 1, 8:16, :], 1, 31))
    flux = y_flux(wall_first, wall_second, 0, 32)
    ey_w = jnp.exp(-(y[0] * y[0]) * half_tw) * quarter_y[0]
    bz_w = rho_w * wall_norm * jnp.exp(-(zed * zed + xi_x * xi_x) * half_tw)
    for iz in range(8):
        b = spread(bz_w[iz : iz + 1])
        flux[2 * iz] = jnp.where(walled, ey_w * b, flux[2 * iz])
        flux[2 * iz + 1] = jnp.where(
            walled, quarter_y[1] * gy[32, pl.ds(iz * 16 + 8, 8), :], flux[2 * iz + 1]
        )
    y_update(31, flux)

    wait_all(vel_copy, 7, ax_f, me)
    for t in range(2):
        fp_ref[pl.ds(8 * t, 8), :] = jnp.where(is_pos, 0.0, fx_ref[pl.ds(8 * t, 8), :])

    @pl.loop(0, N)
    def _(o):
        at_o = (lane == 8 * o + 1) & is_pos
        for t in range(2):
            rows = pl.ds(8 * t, 8)
            fp_ref[rows, :] = jnp.where(
                at_o, pltpu.roll(ax_f[o, rows, :], 8 * o + 1, 1), fp_ref[rows, :]
            )

    quarter_x = 0.25 * abs_x
    fp = (fp_ref[0:8, :], fp_ref[8:16, :])
    even = (lane & 7) == 1

    def packed(t, i):
        return jnp.where(even, spread(fp[t][i : i + 1]), pltpu.roll(spread(fp[t][i + 1 : i + 2]), 4, 1))

    mix, weight, ux, uy = [packed(0, 2 * i) for i in range(4)]
    uz, half = packed(1, 0), packed(1, 2)
    ey = [jnp.exp(-((y[h] - uy) * (y[h] - uy)) * half) for h in range(2)]
    dx = xi_x - ux
    for iz in range(8):
        dz = (iz - 3.5) - uz
        b = quarter_x * weight * jnp.exp(-(dz * dz + dx * dx) * half)
        for h in range(2):
            i = iz * 2 + h
            gpk[i] = (quarter_x * mix) * gpk[i] + ey[h] * b

    @pl.loop(0, N)
    def _(o):
        field = []
        for t in range(2):
            rows = pl.ds(8 * t, 8)
            field.append(
                jnp.where(
                    (lane == 127) & is_pos,
                    pltpu.roll(fx_ref[rows, :], 126 - 8 * o, 1),
                    pltpu.roll(ax_f[o, rows, :], lax.rem(128 - ip, 128), 1),
                )
            )
        for row in range(2):
            r = 2 * o + row
            shift = 126 - 4 * r + ip
            mix, ey, bz = factors(field[0], field[1], row)
            mix = quarter_x * mix
            bz = quarter_x * bz
            for iz in range(8):
                b = spread(bz[iz : iz + 1])
                for h in range(2):
                    at = pl.ds(iz * 16 + h * 8, 8)
                    flux = mix * gx[r, at, :] + ey[h] * b
                    edge = pltpu.roll(gpk[iz * 2 + h], shift, 1)
                    before = jnp.where(at_up, edge, pltpu.roll(flux, step_dn, 1))
                    gx[r, at, :] = fv[r, at, :] - (flux - before)
            pltpu.make_async_copy(gx.at[r], out_hbm.at[:, r], out_sem.at[r]).start()

    wait_all(space_copy, 1, heat, sp)
    piece = lax.broadcasted_iota(jnp.int32, (16, LANES), 0) + sp * 16
    piecef = piece.astype(F32)
    gained = jnp.zeros((16, LANES), F32)
    for k in range(N):
        t = heat[k]
        gained = gained + jnp.where(
            jnp.broadcast_to(t[1:2], (16, LANES)) == piecef,
            jnp.broadcast_to(t[0:1], (16, LANES)),
            0.0,
        )
    gained = jnp.sum(gained, axis=1, keepdims=True)
    own = warm[sp]
    dev = own - 1.0
    before = jnp.where(sp == 0, 0.0, 1.0) * (warm[lax.rem(sp + N - 1, N), 15:16, :] - 1.0)
    after = jnp.where(sp == N - 1, 0.0, 1.0) * (warm[lax.rem(sp + 1, N), 0:1, :] - 1.0)
    dev_before = jnp.concatenate([before, dev[:-1]], axis=0)
    dev_after = jnp.concatenate([dev[1:], after], axis=0)
    new = own + 0.45 * (dev_before - 2.0 * dev + dev_after) + 0.025 * gained
    on_diag = lax.broadcasted_iota(jnp.int32, (16, LANES), 1) == lax.broadcasted_iota(
        jnp.int32, (16, LANES), 0
    )
    row = jnp.sum(jnp.where(on_diag, new, 0.0), axis=0, keepdims=True)
    rev_ref[...] = row[:, :16]

    to_down.wait_send()
    to_up.wait_send()
    for group, buf in enumerate((r1, a1, r32, ry, rx, rex, ay_f, ax_f)):
        wait_all(vel_copy, group, buf, me, ready=False)
    for group, buf in enumerate((warm, heat)):
        wait_all(space_copy, group, buf, sp, ready=False)

    @pl.loop(0, ROWS)
    def _(r):
        pltpu.make_async_copy(gx.at[r], out_hbm.at[:, r], out_sem.at[r]).wait()


def per_device(particle_distribution, piece_warmth, exterior_piece_label):
    tile = functools.partial(pltpu.VMEM, dtype=F32)
    dma = pltpu.SemaphoreType.DMA
    any_spec = pl.BlockSpec(memory_space=pl.ANY)
    vmem_spec = pl.BlockSpec(memory_space=pltpu.VMEM)
    one = tile((N, 8, LANES))
    two = tile((N, 16, LANES))
    out, revised = pl.pallas_call(
        kernel,
        out_shape=(
            jax.ShapeDtypeStruct(particle_distribution.shape, F32),
            jax.ShapeDtypeStruct((1, 16), F32),
        ),
        in_specs=[any_spec, vmem_spec, vmem_spec],
        out_specs=(any_spec, vmem_spec),
        scratch_shapes=[
            tile((ROWS, 128, LANES)), tile((ROWS + 4, 128, LANES)),
            tile((ROWS, 128, LANES)), tile((ROWS + 1, 128, LANES)),
            one, one, two,
            one, one, two,
            one, one, two,
            tile((8, LANES)), one,
            tile((8, LANES)), one,
            two, one,
            one, one, one, one, one, one,
            tile((8, LANES)), tile((16, LANES)), tile((16, LANES)),
            dma((ROWS,)), dma((ROWS,)),
            dma((8, N)), dma((8, N)), dma((3, N)), dma((3, N)),
        ],
        compiler_params=pltpu.CompilerParams(
            collective_id=0, has_side_effects=True, vmem_limit_bytes=24 * 1024 * 1024
        ),
    )(
        particle_distribution,
        piece_warmth.reshape(1, 16),
        exterior_piece_label.reshape(1, LANES),
    )
    return out, revised.reshape(16)


def solution(mesh):
    return jax.shard_map(
        per_device,
        mesh=mesh,
        in_specs=(P("vel", None, "space"), P("space"), P("space")),
        out_specs=(P("vel", None, "space"), P("space")),
        check_vma=False,
    )
```

```python
import functools
import math

import jax
import jax.numpy as jnp
from jax import lax
from jax.experimental import pallas as pl
from jax.experimental.pallas import tpu as pltpu
from jax.sharding import PartitionSpec as P

MESH = pl.DeviceIdType.MESH
N = 16
ROWS = 32
LANES = 128
TWO_PI = 2.0 * math.pi
BITREV = (0, 4, 2, 6, 1, 5, 3, 7)
F32 = jnp.float32


def iota(axis):
    return lax.broadcasted_iota(jnp.int32, (8, LANES), axis)


def spread(row):
    return jnp.broadcast_to(row, (8, LANES))


def minmod(p, q):
    return jnp.maximum(jnp.minimum(p, 0.0), jnp.minimum(jnp.maximum(p, 0.0), q))


def flip8(x, sub):
    x = pltpu.roll(x, 4, 0)
    x = jnp.where((sub & 2) == 0, pltpu.roll(x, 6, 0), pltpu.roll(x, 2, 0))
    return jnp.where((sub & 1) == 0, pltpu.roll(x, 7, 0), pltpu.roll(x, 1, 0))


def merge(a, b, h, sub):
    low = (sub & h) == 0
    if h == 4:
        return jnp.where(low, a, b) + pltpu.roll(jnp.where(low, b, a), 4, 0)
    return jnp.where(low, a, pltpu.roll(b, h, 0)) + jnp.where(
        low, pltpu.roll(a, 8 - h, 0), b
    )


def stack_sums(parts, sub):
    x = [parts[BITREV[i]] for i in range(8)]
    x = [merge(x[2 * i], x[2 * i + 1], 4, sub) for i in range(4)]
    x = [merge(x[2 * i], x[2 * i + 1], 2, sub) for i in range(2)]
    return merge(x[0], x[1], 1, sub)


def z_sums(v):
    s = [v[4 + j] + v[3 - j] for j in range(4)]
    d = [v[4 + j] - v[3 - j] for j in range(4)]
    total = (s[0] + s[1]) + (s[2] + s[3])
    first = (0.5 * d[0] + 1.5 * d[1]) + (2.5 * d[2] + 3.5 * d[3])
    second = (0.25 * s[0] + 2.25 * s[1]) + (6.25 * s[2] + 12.25 * s[3])
    return total, first, second


def quads(low, high, y):
    s0, z0, zz0 = z_sums(low)
    s1, z1, zz1 = z_sums(high)
    a0, a1 = y[0] * s0, y[1] * s1
    return (s0 + s1, a0 + a1, z0 + z1, (y[0] * a0 + y[1] * a1) + (zz0 + zz1)), (
        a1,
        y[1] * (y[1] * a1 + zz1),
    )


def gas(total, by_x, by_xx, sub, face):
    s0 = total
    ux = by_x / s0
    uy = pltpu.roll(total, 6, 0) / s0
    uz = pltpu.roll(total, 4, 0) / s0
    rho = 0.25 * s0
    temp = ((by_xx + pltpu.roll(total, 2, 0)) / s0 - (ux * ux + uy * uy + uz * uz)) / 3.0
    tau = 8.0 * jnp.exp(-0.19 * jnp.log(temp)) / rho
    if face:
        mix = 2.0 * tau / (2.0 * tau + 0.125)
        share = 0.125 / (2.0 * tau + 0.125)
    else:
        mix = (2.0 * tau - 0.125) / (2.0 * tau + 0.25)
        share = 0.375 / (2.0 * tau + 0.25)
    weight = share * rho * jnp.exp(-1.5 * jnp.log(TWO_PI * temp))
    half = 0.5 / temp
    first = jnp.where(
        sub < 2,
        mix,
        jnp.where(
            sub < 4,
            pltpu.roll(weight, 2, 0),
            jnp.where(sub < 6, pltpu.roll(ux, 4, 0), pltpu.roll(uy, 6, 0)),
        ),
    )
    second = jnp.where(sub < 2, uz, pltpu.roll(half, 2, 0))
    return first, second


def gather_sums(ref):
    total = by_x = by_xx = None
    for k in range(N):
        x = 0.5 * (k - 7.5)
        t = ref[k]
        if k == 0:
            total, by_x, by_xx = t, x * t, (x * x) * t
        else:
            total, by_x, by_xx = total + t, by_x + x * t, by_xx + (x * x) * t
    return total, by_x, by_xx


def factors(first, second, row, y, zed, xi_x):
    mix = spread(first[0 + row : 1 + row])
    weight = spread(first[2 + row : 3 + row])
    ux = spread(first[4 + row : 5 + row])
    uy = spread(first[6 + row : 7 + row])
    uz = spread(second[0 + row : 1 + row])
    half = spread(second[2 + row : 3 + row])
    ey = [jnp.exp(-((y[h] - uy) * (y[h] - uy)) * half) for h in range(2)]
    dz, dx = zed - uz, xi_x - ux
    bz = weight * jnp.exp(-(dz * dz + dx * dx) * half)
    return mix, ey, bz


def velocities():
    subf = iota(0).astype(F32)
    return (0.5 * (subf - 7.5), 0.5 * (subf + 0.5)), subf - 3.5


def y_flux(first, second, row, g, j, xi_x):
    y, zed = velocities()
    mix, ey, bz = factors(first, second, row, y, zed, xi_x)
    out = []
    mixed = [mix * (0.25 * y[h]) for h in range(2)]
    eyed = [ey[h] * (0.25 * y[h]) for h in range(2)]
    for iz in range(8):
        b = spread(bz[iz : iz + 1])
        for h in range(2):
            out.append(mixed[h] * g[j, pl.ds(iz * 16 + h * 8, 8), :] + eyed[h] * b)
    return out


def kernel(
    f_hbm, pw_hbm, lab_hbm,
    out_hbm, rev_hbm,
    fv, gy, ay, wf, rev_ref, plus, gx, pw_ref, lab_ref,
    s1, r1, a1, sx, rx, ax, sy, ry, s32, r32, sex, rex, shs, rhs,
    warm, heat, pk, pku, pkd, hf, cpk, gpk, x8_ref, fx_ref, fp_ref, prev,
    in_sem, out_sem, send, recv, arrive, hsend, hrecv,
):
    me = lax.axis_index("vel")
    sp = lax.axis_index("space")
    ip = (me >= 8).astype(jnp.int32)
    dirn = 2 * ip - 1
    xi_x = 0.5 * (me.astype(F32) - 7.5)
    abs_x = xi_x * dirn.astype(F32)
    sub, lane = iota(0), iota(1)
    y, zed = velocities()
    step_dn = lax.rem(dirn + 128, 128)
    step_up = lax.rem(128 - dirn, 128)
    at_up = lane == 127 - 127 * ip
    at_dn = lane == 127 * ip
    is_pos = lane < 128 * ip
    zero = jnp.zeros((8, LANES), F32)

    def far(i):
        half = i // 2
        return 8 + jnp.where(lax.rem(i, 2) == 0, -half, half)

    def near(i):
        half = (i + 1) // 2
        return lax.rem(jnp.where(lax.rem(i, 2) == 0, N - half, half), N)

    def vel_copy(group, d, src, dst, each=None):
        return pltpu.make_async_remote_copy(
            src, dst, send.at[group], recv.at[group] if each is None else arrive.at[each, d],
            device_id={"vel": lax.rem(me + d, N)}, device_id_type=MESH,
        )

    def space_copy(group, d, src, dst):
        return pltpu.make_async_remote_copy(
            src, dst, hsend.at[group], hrecv.at[group],
            device_id={"space": lax.rem(sp + d, N)}, device_id_type=MESH,
        )

    def drain(sem, buf):
        part = buf.at[pl.ds(0, N - 1)]
        pltpu.make_async_copy(part, part, sem).wait()

    def arrival(each, d, buf):
        src = lax.rem(me - d + N, N)
        pltpu.make_async_copy(buf.at[src], buf.at[src], arrive.at[each, d]).wait()

    barrier = pltpu.get_barrier_semaphore()

    @pl.loop(1, N)
    def _(i):
        d = far(i)
        pl.semaphore_signal(
            barrier, 1, device_id={"vel": lax.rem(me + d, N)}, device_id_type=MESH
        )
        pl.semaphore_signal(
            barrier, 1, device_id={"space": lax.rem(sp + d, N)}, device_id_type=MESH
        )

    pw_copy = pltpu.make_async_copy(pw_hbm, pw_ref, in_sem.at[ROWS])
    lab_copy = pltpu.make_async_copy(lab_hbm, lab_ref, in_sem.at[ROWS + 1])
    pw_copy.start()
    lab_copy.start()
    for r in range(ROWS):
        pltpu.make_async_copy(f_hbm.at[:, r], fv.at[r], in_sem.at[r]).start()
    for i in range(16):
        pk[i] = zero

    pw_copy.wait()
    lab_copy.wait()
    own = jnp.broadcast_to(pw_ref[...], (16, 16))
    diag = lax.broadcasted_iota(jnp.int32, (16, 16), 0) == lax.broadcasted_iota(
        jnp.int32, (16, 16), 1
    )
    own = jnp.sum(jnp.where(diag, own, 0.0), axis=1, keepdims=True)
    warm[sp] = jnp.broadcast_to(own, (16, LANES))

    @pl.loop(0, N)
    def _(o):
        parts = [None] * 8
        for row in range(2):
            r = 2 * o + row
            pltpu.make_async_copy(f_hbm.at[:, r], fv.at[r], in_sem.at[r]).wait()
            shift = 4 * r + 2
            mask = (lane >= 4 * r) & (lane <= 4 * r + 3)
            v = [[None] * 8, [None] * 8]
            for iz in range(8):
                for h in range(2):
                    t = fv[r, pl.ds(iz * 16 + h * 8, 8), :]
                    v[h][iz] = t
                    i = iz * 2 + h
                    pk[i] = jnp.where(mask, pltpu.roll(t, shift, 1), pk[i])
            q, _w = quads(v[0], v[1], y)
            for i in range(4):
                parts[2 * i + row] = q[i]
        s1[o] = stack_sums(parts, sub)

    r1[me] = s1[me]
    pl.semaphore_wait(barrier, 2 * (N - 1))

    @pl.loop(1, N)
    def _(i):
        d = far(i)
        vel_copy(0, d, s1.at[lax.rem(me + d, N)], r1.at[me]).start()

    to_down = pltpu.make_async_remote_copy(
        pk, pku, hsend.at[2], hrecv.at[2],
        device_id={"space": lax.rem(sp + dirn + N, N)}, device_id_type=MESH,
    )
    to_up = pltpu.make_async_remote_copy(
        pk, pkd, hsend.at[3], hrecv.at[3],
        device_id={"space": lax.rem(sp - dirn + N, N)}, device_id_type=MESH,
    )
    to_down.start()
    to_up.start()

    @pl.loop(1, N)
    def _(d):
        space_copy(0, d, warm.at[sp], warm.at[sp]).start()

    to_down.wait_recv()
    to_up.wait_recv()
    v = [[None] * 8, [None] * 8]
    w = [[None] * 8, [None] * 8]
    left = ((lane & 2) == 0) == is_pos
    for iz in range(8):
        for h in range(2):
            i = iz * 2 + h
            t = jnp.where(left, pku[i], pkd[i])
            hf[i] = t
            v[h][iz] = t
            w[h][iz] = pk[i]
    q, _w = quads(v[0], v[1], y)
    p, _w = quads(w[0], w[1], y)
    shs[...] = stack_sums([q[0], p[0], q[1], p[1], q[2], p[2], q[3], p[3]], sub)
    rhs[me] = shs[...]

    @pl.loop(1, N)
    def _(i):
        vel_copy(1, far(i), shs, rhs.at[me]).start()

    drain(recv.at[0], r1)
    first, second = gas(*gather_sums(r1), sub, False)
    a1[me, 0:8, :] = first
    a1[me, 8:12, :] = second[0:4]

    @pl.loop(1, N)
    def _(i):
        vel_copy(2, far(i), a1.at[me], a1.at[me], 0).start()

    drain(recv.at[1], rhs)
    first, second = gas(*gather_sums(rhs), sub, False)
    cx = 0.5 - 0.125 * abs_x
    quarter = lane & 3
    centre = quarter == 2 - ip
    across = lax.rem(128 - 2 * dirn, 128)
    sets = []
    for row in range(2):
        mix, weight, ux, uy = [spread(first[2 * i + row : 2 * i + row + 1]) for i in range(4)]
        uz, half = spread(second[row : row + 1]), spread(second[2 + row : 3 + row])
        ey = [jnp.exp(-((y[h] - uy) * (y[h] - uy)) * half) for h in range(2)]
        sets.append((mix, weight, ux - xi_x, uz, half, ey))
    v = [[None] * 8, [None] * 8]
    for iz in range(8):
        b = []
        for mix, weight, dx, uz, half, ey in sets:
            dz = (iz - 3.5) - uz
            b.append(weight * jnp.exp(-(dz * dz + dx * dx) * half))
        for h in range(2):
            i = iz * 2 + h
            u = sets[0][0] * hf[i] + sets[0][5][h] * b[0]
            inside = sets[1][0] * pk[i] + sets[1][5][h] * b[1]
            u2 = pltpu.roll(u, step_dn, 1)
            w0 = pltpu.roll(inside, step_up, 1)
            g = u + cx * minmod(w0 - u, u - u2)
            gpk[i] = g
            v[h][iz] = g
            cpk[i] = jnp.where(centre, u, pltpu.roll(u, across, 1))
    q, _w = quads(v[0], v[1], y)
    parts = [None] * 8
    for k in range(4):
        parts[2 * k] = q[k]
        parts[2 * k + 1] = pltpu.roll(q[k], 124, 1)
    x8 = pltpu.roll(stack_sums(parts, sub), lax.rem(127 + ip, 128), 1)
    x8_ref[...] = x8
    sex[...] = jnp.where(is_pos, 0.0, x8)
    drain(send.at[0], r1)
    drain(send.at[1], rhs)
    to_down.wait_send()
    to_up.wait_send()

    @pl.loop(0, N)
    def _(i):
        d = near(i)
        o = lax.rem(me - d + N, N)

        @pl.when(i > 0)
        def _():
            arrival(0, d, a1)

        first, second = a1[o, 0:8, :], a1[o, 8:12, :]
        parts = [None] * 8
        for row in range(2):
            r = 2 * o + row
            mix, ey, bz = factors(first, second, row, y, zed, xi_x)
            shift = 125 - 4 * r + 2 * ip
            v = [[None] * 8, [None] * 8]
            for iz in range(8):
                b = spread(bz[iz : iz + 1])
                for h in range(2):
                    at = pl.ds(iz * 16 + h * 8, 8)
                    p = mix * fv[r, at, :] + ey[h] * b
                    plus[r + 2, at, :] = p
                    edge = pltpu.roll(cpk[iz * 2 + h], shift, 1)
                    behind = jnp.where(at_up, edge, pltpu.roll(p, step_dn, 1))
                    ahead = jnp.where(at_dn, edge, pltpu.roll(p, step_up, 1))
                    g = p + cx * minmod(ahead - p, p - behind)
                    gx[r, at, :] = g
                    v[h][iz] = g
            q, _w = quads(v[0], v[1], y)
            for k in range(4):
                parts[2 * k + row] = q[k]
        t = stack_sums(parts, sub)
        at_o = (lane == 8 * o + 1) & is_pos
        sex[...] = jnp.where(at_o, pltpu.roll(t, 8 * o + 2, 1), sex[...])
        sx[o] = jnp.where(
            lane < ip, pltpu.roll(x8_ref[...], 127 - 8 * o, 1), pltpu.roll(t, ip, 1)
        )

        @pl.when(i > 0)
        def _():
            vel_copy(3, lax.rem(N - d, N), sx.at[o], rx.at[me]).start()

    rx[me] = sx[me]
    rex[me] = sex[...]

    for ghost, real in ((1, 2), (0, 3), (34, 33), (35, 32)):
        for iz in range(8):
            lo, hi = pl.ds(iz * 16, 8), pl.ds(iz * 16 + 8, 8)
            x0, x1 = plus[real, lo, :], plus[real, hi, :]
            plus[ghost, lo, :] = flip8(x1, sub)
            plus[ghost, hi, :] = flip8(x0, sub)

    cy = (0.5 + 0.125 * y[0], 0.5 - 0.125 * y[1])

    def y_face(j):
        v = [[None] * 8, [None] * 8]
        for iz in range(8):
            for h in range(2):
                at = pl.ds(iz * 16 + h * 8, 8)
                if h:
                    c, b, a = plus[j + 1, at, :], plus[j, at, :], plus[j + 2, at, :]
                else:
                    c, b, a = plus[j + 2, at, :], plus[j + 3, at, :], plus[j + 1, at, :]
                g = c + cy[h] * minmod(a - c, c - b)
                gy[j, at, :] = g
                v[h][iz] = g
        return quads(v[0], v[1], y)

    @pl.loop(0, N)
    def _(i):
        d = lax.rem(far(i + 1), N)
        o = lax.rem(me + d, N)
        parts = [None] * 8
        for row in range(2):
            q, _w = y_face(2 * o + row)
            for k in range(4):
                parts[2 * k + row] = q[k]
        sy[o] = stack_sums(parts, sub)

        @pl.when(d > 0)
        def _():
            vel_copy(4, d, sy.at[o], ry.at[me]).start()

    ry[me] = sy[me]
    q, w = y_face(32)
    s32[...] = stack_sums([q[0], w[0], q[1], w[1], q[2], zero, q[3], zero], sub)
    r32[me] = s32[...]

    @pl.loop(1, N)
    def _(i):
        d = far(i)
        vel_copy(5, d, s32, r32.at[me]).start()
        vel_copy(6, d, sex, rex.at[me]).start()

    @pl.loop(0, ROWS)
    def _(r):
        for i in range(16):
            at = pl.ds(i * 8, 8)
            fv[r, at, :] = (4.0 / 3.0) * plus[r + 2, at, :] - fv[r, at, :] * (1.0 / 3.0)

    drain(send.at[2], a1)
    drain(send.at[3], rx)

    drain(recv.at[3], rx)
    first, second = gas(*gather_sums(rx), sub, True)
    ax[me, 0:8, :] = first
    ax[me, 8:12, :] = second[0:4]

    @pl.loop(1, N)
    def _(i):
        vel_copy(7, far(i), ax.at[me], ax.at[me]).start()

    drain(recv.at[4], ry)
    first, second = gas(*gather_sums(ry), sub, True)
    ay[me, 0:8, :] = first
    ay[me, 8:12, :] = second[0:4]

    @pl.loop(1, N)
    def _(i):
        vel_copy(8, far(i), ay.at[me], ay.at[me]).start()

    drain(hrecv.at[0], warm)
    label = spread(lab_ref[...])
    walled = label >= 0
    tw_sum = zero
    for k in range(N):
        for h in range(2):
            tw_sum = tw_sum + jnp.where(
                label == k * 16 + h * 8 + sub, warm[k, pl.ds(8 * h, 8), :], 0.0
            )
    tw = jnp.where(walled, spread(jnp.sum(tw_sum, axis=0, keepdims=True)), 1.0)
    half_tw = 0.5 / tw
    wall_norm = jnp.exp(-1.5 * jnp.log(TWO_PI * tw))
    e_xy = jnp.exp(-(y[1] * y[1]) * half_tw)
    e_z = jnp.exp(-(zed * zed) * half_tw)

    def down(t):
        return spread(jnp.sum(t, axis=0, keepdims=True))

    sum_x, sum_xx = 2.0 * down(e_xy), 2.0 * down(y[1] * y[1] * e_xy)
    sum_z, sum_zz = down(e_z), down(zed * zed * e_z)
    sum_y1, sum_y3 = down(y[1] * e_xy), down(y[1] * y[1] * y[1] * e_xy)
    out_mass = wall_norm * (sum_x * sum_z * sum_y1)
    out_energy = 0.5 * wall_norm * (
        sum_xx * sum_z * sum_y1 + sum_x * sum_zz * sum_y1 + sum_x * sum_z * sum_y3
    )

    drain(recv.at[5], r32)
    total, by_x, by_xx = gather_sums(r32)
    wall_first, wall_second = gas(total, by_x, by_xx, sub, True)
    in_mass = spread(total[1:2])
    in_energy = 0.5 * spread(by_xx[1:2] + total[3:4])
    rho_w = in_mass / out_mass
    flow = jnp.where(walled, 0.25 * (in_energy - rho_w * out_energy), 0.0)
    heat[sp] = jnp.where(sub == 0, flow, label.astype(F32))

    @pl.loop(1, N)
    def _(d):
        space_copy(1, d, heat.at[sp], heat.at[sp]).start()

    flux = y_flux(wall_first, wall_second, 0, gy, 32, xi_x)
    ey_w = jnp.exp(-(y[0] * y[0]) * half_tw) * (0.25 * y[0])
    bz_w = rho_w * wall_norm * jnp.exp(-(zed * zed + xi_x * xi_x) * half_tw)
    for iz in range(8):
        b = spread(bz_w[iz : iz + 1])
        wf[2 * iz] = jnp.where(walled, ey_w * b, flux[2 * iz])
        wf[2 * iz + 1] = jnp.where(
            walled, (0.25 * y[1]) * gy[32, pl.ds(iz * 16 + 8, 8), :], flux[2 * iz + 1]
        )

    drain(recv.at[6], rex)
    fx_first, fx_second = gas(*gather_sums(rex), sub, True)
    fx_ref[0:8, :] = fx_first
    fx_ref[8:16, :] = fx_second
    drain(send.at[4], ry)
    drain(send.at[5], r32)
    drain(send.at[6], rex)
    drain(hsend.at[0], warm)

    drain(recv.at[7], ax)
    fp_ref[0:8, :] = jnp.where(is_pos, 0.0, fx_ref[0:8, :])
    fp_ref[8:12, :] = jnp.where(is_pos[0:4], 0.0, fx_ref[8:12, :])

    @pl.loop(0, N)
    def _(o):
        at_o = (lane == 8 * o + 1) & is_pos
        for lo, hi in ((0, 8), (8, 12)):
            fp_ref[lo:hi, :] = jnp.where(
                at_o[0 : hi - lo], pltpu.roll(ax[o, lo:hi, :], 8 * o + 1, 1), fp_ref[lo:hi, :]
            )

    quarter_x = 0.25 * abs_x
    fp = pltpu.roll(fp_ref[...], 1 - ip, 1)
    even = (lane & 7) == 2 - ip

    def packed(i):
        return jnp.where(
            even, spread(fp[i : i + 1]), pltpu.roll(spread(fp[i + 1 : i + 2]), 4, 1)
        )

    mix, weight, ux, uy, uz, half = [packed(2 * i) for i in range(6)]
    ey = [jnp.exp(-((y[h] - uy) * (y[h] - uy)) * half) for h in range(2)]
    dx = xi_x - ux
    for iz in range(8):
        dz = (iz - 3.5) - uz
        b = quarter_x * weight * jnp.exp(-(dz * dz + dx * dx) * half)
        for h in range(2):
            i = iz * 2 + h
            gpk[i] = (quarter_x * mix) * gpk[i] + ey[h] * b

    @pl.loop(0, N)
    def _(o):
        field = []
        for lo, hi in ((0, 8), (8, 12)):
            field.append(
                jnp.where(
                    ((lane == 127) & is_pos)[0 : hi - lo],
                    pltpu.roll(fx_ref[lo:hi, :], 126 - 8 * o, 1),
                    pltpu.roll(ax[o, lo:hi, :], lax.rem(128 - ip, 128), 1),
                )
            )
        for row in range(2):
            r = 2 * o + row
            shift = 125 - 4 * r + 2 * ip
            mix, ey, bz = factors(field[0], field[1], row, y, zed, xi_x)
            mix = quarter_x * mix
            bz = quarter_x * bz
            for iz in range(8):
                b = spread(bz[iz : iz + 1])
                for h in range(2):
                    at = pl.ds(iz * 16 + h * 8, 8)
                    flux = mix * gx[r, at, :] + ey[h] * b
                    edge = pltpu.roll(gpk[iz * 2 + h], shift, 1)
                    before = jnp.where(at_up, edge, pltpu.roll(flux, step_dn, 1))
                    fv[r, at, :] = fv[r, at, :] - (flux - before)

    drain(hrecv.at[1], heat)
    piece = lax.broadcasted_iota(jnp.int32, (16, LANES), 0) + sp * 16
    piecef = piece.astype(F32)
    gained = jnp.zeros((16, LANES), F32)
    for k in range(N):
        t = heat[k]
        gained = gained + jnp.where(
            jnp.broadcast_to(t[1:2], (16, LANES)) == piecef,
            jnp.broadcast_to(t[0:1], (16, LANES)),
            0.0,
        )
    gained = jnp.sum(gained, axis=1, keepdims=True)
    own = warm[sp]
    dev = own - 1.0
    before = jnp.where(sp == 0, 0.0, 1.0) * (warm[lax.rem(sp + N - 1, N), 15:16, :] - 1.0)
    after = jnp.where(sp == N - 1, 0.0, 1.0) * (warm[lax.rem(sp + 1, N), 0:1, :] - 1.0)
    dev_before = jnp.concatenate([before, dev[:-1]], axis=0)
    dev_after = jnp.concatenate([dev[1:], after], axis=0)
    new = own + 0.45 * (dev_before - 2.0 * dev + dev_after) + 0.025 * gained
    on_diag = lax.broadcasted_iota(jnp.int32, (16, LANES), 1) == lax.broadcasted_iota(
        jnp.int32, (16, LANES), 0
    )
    rev_ref[...] = jnp.sum(jnp.where(on_diag, new, 0.0), axis=0, keepdims=True)[:, 0:16]

    rev_copy = pltpu.make_async_copy(rev_ref, rev_hbm, out_sem.at[ROWS])
    rev_copy.start()
    drain(send.at[7], ax)
    drain(hsend.at[1], heat)

    drain(recv.at[8], ay)
    def update(r, flux):
        for i in range(16):
            at = pl.ds(i * 8, 8)
            gx[r, at, :] = fv[r, at, :] - (flux[i] - prev[i])
            prev[i] = flux[i]
        pltpu.make_async_copy(gx.at[r], out_hbm.at[:, r], out_sem.at[r]).start()

    def face(o, row):
        return y_flux(ay[o, 0:8, :], ay[o, 8:12, :], row, gy, 2 * o + row, xi_x)

    flux = face(0, 0)
    for i in range(16):
        prev[i] = flux[i]

    @pl.loop(0, N - 1)
    def _(o):
        update(2 * o, face(o, 1))
        update(2 * o + 1, face(o + 1, 0))

    update(30, face(N - 1, 1))
    update(31, [wf[i] for i in range(16)])
    drain(send.at[8], ay)
    rev_copy.wait()

    @pl.loop(0, ROWS)
    def _(r):
        pltpu.make_async_copy(gx.at[r], out_hbm.at[:, r], out_sem.at[r]).wait()


def per_device(particle_distribution, piece_warmth, exterior_piece_label):
    tile = functools.partial(pltpu.VMEM, dtype=F32)
    dma = pltpu.SemaphoreType.DMA
    hbm = pl.BlockSpec(memory_space=pltpu.HBM)
    one = tile((N, 8, LANES))
    two = tile((N, 12, LANES))
    flat = tile((8, LANES))
    shape = functools.partial(jax.ShapeDtypeStruct, dtype=F32)
    out, revised = pl.pallas_call(
        kernel,
        out_shape=(shape(particle_distribution.shape), shape((1, 16))),
        in_specs=[hbm] * 3,
        out_specs=(hbm, hbm),
        scratch_shapes=[
            tile((ROWS, 128, LANES)), tile((ROWS + 1, 128, LANES)), two, one, tile((1, 16)),
            tile((ROWS + 4, 128, LANES)), tile((ROWS, 128, LANES)),
            tile((1, 16)), pltpu.VMEM((1, LANES), jnp.int32),
            one, one, two,
            one, one, two,
            one, one,
            flat, one,
            flat, one,
            flat, one,
            tile((N, 16, LANES)), one,
            one, one, one, one, one, one,
            flat, tile((16, LANES)), tile((12, LANES)), one,
            dma((ROWS + 2,)), dma((ROWS + 1,)),
            dma((9,)), dma((9,)), dma((1, N)), dma((4,)), dma((4,)),
        ],
        compiler_params=pltpu.CompilerParams(
            collective_id=0, has_side_effects=True, vmem_limit_bytes=62 * 1024 * 1000
        ),
    )(
        particle_distribution,
        piece_warmth.reshape(1, 16),
        exterior_piece_label.reshape(1, LANES),
    )
    return out, revised.reshape(16)


def solution(mesh):
    return jax.shard_map(
        per_device,
        mesh=mesh,
        in_specs=(P("vel", None, "space"), P("space"), P("space")),
        out_specs=(P("vel", None, "space"), P("space")),
        check_vma=False,
    )
```

```python
import functools
import math

import jax
import jax.numpy as jnp
from jax import lax
from jax.experimental import pallas as pl
from jax.experimental.pallas import tpu as pltpu
from jax.sharding import PartitionSpec as P

MESH = pl.DeviceIdType.MESH
N = 16
ROWS = 32
LANES = 128
TWO_PI = 2.0 * math.pi
BITREV = (0, 4, 2, 6, 1, 5, 3, 7)
F32 = jnp.float32


def iota(axis):
    return lax.broadcasted_iota(jnp.int32, (8, LANES), axis)


def spread(row):
    return jnp.broadcast_to(row, (8, LANES))


def minmod(p, q):
    return jnp.maximum(jnp.minimum(p, 0.0), jnp.minimum(jnp.maximum(p, 0.0), q))


def flip8(x, sub):
    x = pltpu.roll(x, 4, 0)
    x = jnp.where((sub & 2) == 0, pltpu.roll(x, 6, 0), pltpu.roll(x, 2, 0))
    return jnp.where((sub & 1) == 0, pltpu.roll(x, 7, 0), pltpu.roll(x, 1, 0))


def merge(a, b, h, sub):
    low = (sub & h) == 0
    if h == 4:
        return jnp.where(low, a, b) + pltpu.roll(jnp.where(low, b, a), 4, 0)
    return jnp.where(low, a, pltpu.roll(b, h, 0)) + jnp.where(
        low, pltpu.roll(a, 8 - h, 0), b
    )


def stack_sums(parts, sub):
    x = [parts[BITREV[i]] for i in range(8)]
    x = [merge(x[2 * i], x[2 * i + 1], 4, sub) for i in range(4)]
    x = [merge(x[2 * i], x[2 * i + 1], 2, sub) for i in range(2)]
    return merge(x[0], x[1], 1, sub)


def z_sums(v):
    s = [v[4 + j] + v[3 - j] for j in range(4)]
    d = [v[4 + j] - v[3 - j] for j in range(4)]
    total = (s[0] + s[1]) + (s[2] + s[3])
    first = (0.5 * d[0] + 1.5 * d[1]) + (2.5 * d[2] + 3.5 * d[3])
    second = (0.25 * s[0] + 2.25 * s[1]) + (6.25 * s[2] + 12.25 * s[3])
    return total, first, second


def quads(low, high, y):
    s0, z0, zz0 = z_sums(low)
    s1, z1, zz1 = z_sums(high)
    a0, a1 = y[0] * s0, y[1] * s1
    return (s0 + s1, a0 + a1, z0 + z1, (y[0] * a0 + y[1] * a1) + (zz0 + zz1)), (
        a1,
        y[1] * (y[1] * a1 + zz1),
    )


def gas(total, by_x, by_xx, sub, face):
    s0 = total
    ux = by_x / s0
    uy = pltpu.roll(total, 6, 0) / s0
    uz = pltpu.roll(total, 4, 0) / s0
    rho = 0.25 * s0
    temp = ((by_xx + pltpu.roll(total, 2, 0)) / s0 - (ux * ux + uy * uy + uz * uz)) / 3.0
    tau = 8.0 * jnp.exp(-0.19 * jnp.log(temp)) / rho
    if face:
        mix = 2.0 * tau / (2.0 * tau + 0.125)
        share = 0.125 / (2.0 * tau + 0.125)
    else:
        mix = (2.0 * tau - 0.125) / (2.0 * tau + 0.25)
        share = 0.375 / (2.0 * tau + 0.25)
    weight = share * rho * jnp.exp(-1.5 * jnp.log(TWO_PI * temp))
    half = 0.5 / temp
    first = jnp.where(
        sub < 2,
        mix,
        jnp.where(
            sub < 4,
            pltpu.roll(weight, 2, 0),
            jnp.where(sub < 6, pltpu.roll(ux, 4, 0), pltpu.roll(uy, 6, 0)),
        ),
    )
    second = jnp.where(sub < 2, uz, pltpu.roll(half, 2, 0))
    return first, second


def gather_sums(ref):
    total = by_x = by_xx = None
    for k in range(N):
        x = 0.5 * (k - 7.5)
        t = ref[k]
        if k == 0:
            total, by_x, by_xx = t, x * t, (x * x) * t
        else:
            total, by_x, by_xx = total + t, by_x + x * t, by_xx + (x * x) * t
    return total, by_x, by_xx


def factors(first, second, row, y, zed, xi_x):
    mix = spread(first[0 + row : 1 + row])
    weight = spread(first[2 + row : 3 + row])
    ux = spread(first[4 + row : 5 + row])
    uy = spread(first[6 + row : 7 + row])
    uz = spread(second[0 + row : 1 + row])
    half = spread(second[2 + row : 3 + row])
    ey = [jnp.exp(-((y[h] - uy) * (y[h] - uy)) * half) for h in range(2)]
    dz, dx = zed - uz, xi_x - ux
    bz = weight * jnp.exp(-(dz * dz + dx * dx) * half)
    return mix, ey, bz


def velocities():
    subf = iota(0).astype(F32)
    return (0.5 * (subf - 7.5), 0.5 * (subf + 0.5)), subf - 3.5


def y_flux(first, second, row, g, j, xi_x):
    y, zed = velocities()
    mix, ey, bz = factors(first, second, row, y, zed, xi_x)
    out = []
    mixed = [mix * (0.25 * y[h]) for h in range(2)]
    eyed = [ey[h] * (0.25 * y[h]) for h in range(2)]
    for iz in range(8):
        b = spread(bz[iz : iz + 1])
        for h in range(2):
            out.append(mixed[h] * g[j, pl.ds(iz * 16 + h * 8, 8), :] + eyed[h] * b)
    return out


def kernel(
    f_hbm, pw_hbm, lab_hbm,
    out_hbm, rev_hbm,
    fv, gy, ay, wf, rev_ref, plus, gx, pw_ref, lab_ref,
    s1, r1, a1, sx, rx, ax, sy, ry, s32, r32, sex, rex, shs, rhs,
    warm, heat, pk, pku, pkd, hf, ge, gh, slots, fresh,
    in_sem, out_sem, send, recv, arrive, hsend, hrecv,
):
    me = lax.axis_index("vel")
    sp = lax.axis_index("space")
    ip = (me >= 8).astype(jnp.int32)
    dirn = 2 * ip - 1
    xi_x = 0.5 * (me.astype(F32) - 7.5)
    cx = 0.5 * dirn.astype(F32) - 0.125 * xi_x
    sub, lane = iota(0), iota(1)
    y, zed = velocities()
    is_pos = lane < 128 * ip
    at_edge = (lane == 0) | (lane == 127 - 126 * ip)
    zero = jnp.zeros((8, LANES), F32)

    def far(i):
        half = i // 2
        return 8 + jnp.where(lax.rem(i, 2) == 0, -half, half)

    def near(i):
        half = (i + 1) // 2
        return lax.rem(jnp.where(lax.rem(i, 2) == 0, N - half, half), N)

    def vel_copy(group, d, src, dst, each=None):
        return pltpu.make_async_remote_copy(
            src, dst, send.at[group], recv.at[group] if each is None else arrive.at[each, d],
            device_id={"vel": lax.rem(me + d, N)}, device_id_type=MESH,
        )

    def space_copy(group, d, src, dst):
        return pltpu.make_async_remote_copy(
            src, dst, hsend.at[group], hrecv.at[group],
            device_id={"space": lax.rem(sp + d, N)}, device_id_type=MESH,
        )

    def drain(sem, buf):
        part = buf.at[pl.ds(0, N - 1)]
        pltpu.make_async_copy(part, part, sem).wait()

    def arrival(each, d, buf):
        src = lax.rem(me - d + N, N)
        pltpu.make_async_copy(buf.at[src], buf.at[src], arrive.at[each, d]).wait()

    def load16(ref, r):
        return [
            [ref[r, pl.ds(iz * 16 + h * 8, 8), :] for iz in range(8)] for h in range(2)
        ]

    barrier = pltpu.get_barrier_semaphore()

    @pl.loop(1, N)
    def _(i):
        d = far(i)
        pl.semaphore_signal(
            barrier, 1, device_id={"vel": lax.rem(me + d, N)}, device_id_type=MESH
        )
        pl.semaphore_signal(
            barrier, 1, device_id={"space": lax.rem(sp + d, N)}, device_id_type=MESH
        )

    for r in range(ROWS):
        pltpu.make_async_copy(f_hbm.at[:, r], fv.at[r], in_sem.at[r]).start()
    pw_copy = pltpu.make_async_copy(pw_hbm, pw_ref, in_sem.at[ROWS])
    lab_copy = pltpu.make_async_copy(lab_hbm, lab_ref, in_sem.at[ROWS + 1])
    pw_copy.start()
    lab_copy.start()

    for i in range(16):
        pk[i] = zero

    @pl.loop(0, N)
    def _(o):
        parts = [None] * 8
        edge = [pk[i] for i in range(16)]
        for row in range(2):
            r = 2 * o + row
            pltpu.make_async_copy(f_hbm.at[:, r], fv.at[r], in_sem.at[r]).wait()
        for row in range(2):
            r = 2 * o + row
            v = load16(fv, r)
            mask = (lane >= 4 * r) & (lane <= 4 * r + 3)
            for i in range(16):
                edge[i] = jnp.where(mask, pltpu.roll(v[i % 2][i // 2], 4 * r + 2, 1), edge[i])
            q, _w = quads(v[0], v[1], y)
            for i in range(4):
                parts[2 * i + row] = q[i]
        for i in range(16):
            pk[i] = edge[i]
        s1[o] = stack_sums(parts, sub)

    r1[me] = s1[me]
    pl.semaphore_wait(barrier, 2 * (N - 1))

    @pl.loop(1, N)
    def _(i):
        d = far(i)
        vel_copy(0, d, s1.at[lax.rem(me + d, N)], r1.at[me]).start()

    to_right = pltpu.make_async_remote_copy(
        pk, pku, hsend.at[2], hrecv.at[2],
        device_id={"space": lax.rem(sp + 1, N)}, device_id_type=MESH,
    )
    to_left = pltpu.make_async_remote_copy(
        pk, pkd, hsend.at[3], hrecv.at[3],
        device_id={"space": lax.rem(sp + N - 1, N)}, device_id_type=MESH,
    )
    to_right.start()
    to_left.start()

    drain(recv.at[0], r1)
    first, second = gas(*gather_sums(r1), sub, False)
    a1[me, 0:8, :] = first
    a1[me, 8:12, :] = second[0:4]

    @pl.loop(1, N)
    def _(i):
        vel_copy(2, far(i), a1.at[me], a1.at[me], 0).start()

    to_right.wait_recv()
    to_left.wait_recv()
    v = [[None] * 8, [None] * 8]
    w = [[None] * 8, [None] * 8]
    for iz in range(8):
        for h in range(2):
            i = iz * 2 + h
            t = jnp.where((lane & 2) == 0, pku[i], pkd[i])
            hf[i] = t
            v[h][iz] = t
            w[h][iz] = pk[i]
    q, _w = quads(v[0], v[1], y)
    p, _w = quads(w[0], w[1], y)
    shs[...] = stack_sums([q[0], p[0], q[1], p[1], q[2], p[2], q[3], p[3]], sub)
    rhs[me] = shs[...]

    @pl.loop(1, N)
    def _(i):
        vel_copy(1, far(i), shs, rhs.at[me]).start()

    pw_copy.wait()
    lab_copy.wait()
    warm[sp, :, 0:16] = pw_ref[...]

    @pl.loop(1, N)
    def _(d):
        space_copy(0, d, warm.at[sp], warm.at[sp]).start()

    drain(send.at[0], r1)

    def owner(i):
        return lax.rem(me - near(i) + N, N)

    def half_step(i, slot):
        o = owner(i)
        first, second = a1[o, 0:8, :], a1[o, 8:12, :]
        for row in range(2):
            r = 2 * o + row
            mix, ey, bz = factors(first, second, row, y, zed, xi_x)
            for iz in range(8):
                b = spread(bz[iz : iz + 1])
                for h in range(2):
                    at = pl.ds(iz * 16 + h * 8, 8)
                    p = mix * fv[r, at, :] + ey[h] * b
                    plus[r + 2, at, :] = p
                    fresh[slot, row, at, :] = p

    def rolls(slot):
        for row in range(2):
            for k in range(16):
                at = pl.ds(k * 8, 8)
                p = fresh[slot, row, at, :]
                slots[slot, 0, row, at, :] = p
                slots[slot, 1, row, at, :] = pltpu.roll(p, 1, 1)
                slots[slot, 2, row, at, :] = pltpu.roll(p, 127, 1)

    def x_faces(i, slot):
        o = owner(i)
        parts = [None] * 8
        for row in range(2):
            r = 2 * o + row
            v = [[None] * 8, [None] * 8]
            for iz in range(8):
                for h in range(2):
                    at = pl.ds(iz * 16 + h * 8, 8)
                    p = slots[slot, 0, row, at, :]
                    g = p + cx * minmod(
                        slots[slot, 2, row, at, :] - p, p - slots[slot, 1, row, at, :]
                    )
                    gx[r, at, :] = g
                    v[h][iz] = g
            q, _w = quads(v[0], v[1], y)
            for k in range(4):
                parts[2 * k + row] = q[k]
        sx[o] = stack_sums(parts, sub)

    half_step(0, 0)
    arrival(0, near(1), a1)
    rolls(0)
    half_step(1, 1)

    @pl.loop(1, 8)
    def _(k):
        i = 2 * k
        arrival(0, near(i), a1)
        rolls(1)
        half_step(i, 0)
        x_faces(i - 2, 0)
        arrival(0, near(i + 1), a1)
        rolls(0)
        half_step(i + 1, 1)
        x_faces(i - 1, 1)

    rolls(1)
    x_faces(14, 0)
    x_faces(15, 1)

    for ghost, real in ((1, 2), (0, 3), (34, 33), (35, 32)):
        for iz in range(8):
            lo, hi = pl.ds(iz * 16, 8), pl.ds(iz * 16 + 8, 8)
            x0, x1 = plus[real, lo, :], plus[real, hi, :]
            plus[ghost, lo, :] = flip8(x1, sub)
            plus[ghost, hi, :] = flip8(x0, sub)

    cy = (0.5 + 0.125 * y[0], 0.5 - 0.125 * y[1])

    def y_face(j):
        v = [[None] * 8, [None] * 8]
        for iz in range(8):
            for h in range(2):
                at = pl.ds(iz * 16 + h * 8, 8)
                if h:
                    c, b, a = plus[j + 1, at, :], plus[j, at, :], plus[j + 2, at, :]
                else:
                    c, b, a = plus[j + 2, at, :], plus[j + 3, at, :], plus[j + 1, at, :]
                g = c + cy[h] * minmod(a - c, c - b)
                gy[j, at, :] = g
                v[h][iz] = g
        return quads(v[0], v[1], y)

    @pl.loop(0, N)
    def _(i):
        d = lax.rem(far(i + 1), N)
        o = lax.rem(me + d, N)
        parts = [None] * 8
        for row in range(2):
            q, _w = y_face(2 * o + row)
            for k in range(4):
                parts[2 * k + row] = q[k]
        sy[o] = stack_sums(parts, sub)

        @pl.when(d > 0)
        def _():
            vel_copy(4, d, sy.at[o], ry.at[me]).start()

    ry[me] = sy[me]
    q, w = y_face(32)
    s32[...] = stack_sums([q[0], w[0], q[1], w[1], q[2], zero, q[3], zero], sub)
    r32[me] = s32[...]

    drain(recv.at[1], rhs)
    first, second = gas(*gather_sums(rhs), sub, False)
    sets = []
    for row in range(2):
        mix, weight, ux, uy = [spread(first[2 * i + row : 2 * i + row + 1]) for i in range(4)]
        uz, half = spread(second[row : row + 1]), spread(second[2 + row : 3 + row])
        ey = [jnp.exp(-((y[h] - uy) * (y[h] - uy)) * half) for h in range(2)]
        sets.append((mix, weight, ux - xi_x, uz, half, ey))
    v = [[None] * 8, [None] * 8]
    w = [[None] * 8, [None] * 8]
    at_one = (lane & 3) == 1
    for iz in range(8):
        b = []
        for mix, weight, dx, uz, half, ey in sets:
            dz = (iz - 3.5) - uz
            b.append(weight * jnp.exp(-(dz * dz + dx * dx) * half))
        for h in range(2):
            i = iz * 2 + h
            u = sets[0][0] * hf[i] + sets[0][5][h] * b[0]
            p = sets[1][0] * pk[i] + sets[1][5][h] * b[1]
            ul, pl_ = pltpu.roll(u, 1, 1), pltpu.roll(p, 1, 1)
            ur, pr = pltpu.roll(u, 127, 1), pltpu.roll(p, 127, 1)
            inner = p + cx * minmod(
                jnp.where(at_one, ur, pr) - p, p - jnp.where(at_one, pl_, ul)
            )
            outer = u + cx * minmod(
                jnp.where(at_one, pr, ur) - u, u - jnp.where(at_one, ul, pl_)
            )
            ge[i] = inner
            gh[i] = outer
            v[h][iz] = inner
            w[h][iz] = outer

    def packed_tile(v):
        q, _w = quads(v[0], v[1], y)
        parts = [None] * 8
        for k in range(4):
            parts[2 * k] = q[k]
            parts[2 * k + 1] = pltpu.roll(q[k], 124, 1)
        return stack_sums(parts, sub)

    inner, outer = packed_tile(v), packed_tile(w)
    sex[...] = jnp.where(is_pos, inner, pltpu.roll(outer, 127, 1))
    edges = jnp.where(is_pos & ((lane & 7) == 1), outer, inner)

    @pl.loop(0, N)
    def _(i):
        d = lax.rem(far(i + 1), N)
        o = lax.rem(me + d, N)
        sx[o] = jnp.where(
            at_edge, pltpu.roll(edges, 126 - 8 * o + ip, 1), pltpu.roll(sx[o], ip, 1)
        )

        @pl.when(d > 0)
        def _():
            vel_copy(3, d, sx.at[o], rx.at[me]).start()

    rx[me] = sx[me]
    rex[me] = sex[...]

    @pl.loop(1, N)
    def _(i):
        d = far(i)
        vel_copy(5, d, s32, r32.at[me]).start()
        vel_copy(6, d, sex, rex.at[me]).start()

    @pl.loop(0, N)
    def _(o):
        for i in range(16):
            at = pl.ds(i * 8, 8)
            e = jnp.where(is_pos & at_one, gh[i], ge[i])
            for row in range(2):
                r = 2 * o + row
                gx[r, at, :] = jnp.where(
                    at_edge,
                    pltpu.roll(e, 126 - 4 * r + ip, 1),
                    pltpu.roll(gx[r, at, :], ip, 1),
                )

    @pl.loop(0, ROWS)
    def _(r):
        for i in range(16):
            at = pl.ds(i * 8, 8)
            fv[r, at, :] = (4.0 / 3.0) * plus[r + 2, at, :] - fv[r, at, :] * (1.0 / 3.0)

    drain(hrecv.at[0], warm)
    label = spread(lab_ref[...])
    walled = label >= 0
    by_lane = lax.broadcasted_iota(jnp.int32, (16, LANES), 1)
    by_row = lax.broadcasted_iota(jnp.int32, (16, LANES), 0)
    on_diag = by_lane == by_row

    def column(k):
        return jnp.sum(
            jnp.where(on_diag, jnp.broadcast_to(warm[k], (16, LANES)), 0.0),
            axis=1, keepdims=True,
        )

    tw_sum = jnp.zeros((16, LANES), F32)
    label16 = jnp.broadcast_to(lab_ref[...], (16, LANES))
    for k in range(N):
        tw_sum = tw_sum + jnp.where(label16 == k * 16 + by_row, column(k), 0.0)
    tw_sum = tw_sum[0:8] + tw_sum[8:16]
    tw = jnp.where(walled, spread(jnp.sum(tw_sum, axis=0, keepdims=True)), 1.0)
    half_tw = 0.5 / tw
    wall_norm = jnp.exp(-1.5 * jnp.log(TWO_PI * tw))
    e_xy = jnp.exp(-(y[1] * y[1]) * half_tw)
    e_z = jnp.exp(-(zed * zed) * half_tw)

    def down(t):
        return spread(jnp.sum(t, axis=0, keepdims=True))

    sum_x, sum_xx = 2.0 * down(e_xy), 2.0 * down(y[1] * y[1] * e_xy)
    sum_z, sum_zz = down(e_z), down(zed * zed * e_z)
    sum_y1, sum_y3 = down(y[1] * e_xy), down(y[1] * y[1] * y[1] * e_xy)
    out_mass = wall_norm * (sum_x * sum_z * sum_y1)
    out_energy = 0.5 * wall_norm * (
        sum_xx * sum_z * sum_y1 + sum_x * sum_zz * sum_y1 + sum_x * sum_z * sum_y3
    )

    drain(send.at[1], rhs)
    drain(send.at[2], a1)
    to_right.wait_send()
    to_left.wait_send()

    drain(recv.at[4], ry)
    first, second = gas(*gather_sums(ry), sub, True)
    ay[me, 0:8, :] = first
    ay[me, 8:12, :] = second[0:4]

    @pl.loop(1, N)
    def _(i):
        vel_copy(8, far(i), ay.at[me], ay.at[me], 1).start()

    drain(recv.at[3], rx)
    first, second = gas(*gather_sums(rx), sub, True)
    ax[me, 0:8, :] = first
    ax[me, 8:12, :] = second[0:4]

    @pl.loop(1, N)
    def _(i):
        vel_copy(7, far(i), ax.at[me], ax.at[me], 2).start()

    drain(recv.at[5], r32)
    total, by_x, by_xx = gather_sums(r32)
    wall_first, wall_second = gas(total, by_x, by_xx, sub, True)
    in_mass = spread(total[1:2])
    in_energy = 0.5 * spread(by_xx[1:2] + total[3:4])
    rho_w = in_mass / out_mass
    flow = jnp.where(walled, 0.25 * (in_energy - rho_w * out_energy), 0.0)
    heat[sp] = jnp.where(sub == 0, flow, label.astype(F32))

    @pl.loop(1, N)
    def _(d):
        space_copy(1, d, heat.at[sp], heat.at[sp]).start()

    flux = y_flux(wall_first, wall_second, 0, gy, 32, xi_x)
    ey_w = jnp.exp(-(y[0] * y[0]) * half_tw) * (0.25 * y[0])
    bz_w = rho_w * wall_norm * jnp.exp(-(zed * zed + xi_x * xi_x) * half_tw)
    for iz in range(8):
        b = spread(bz_w[iz : iz + 1])
        wf[2 * iz] = jnp.where(walled, ey_w * b, flux[2 * iz])
        wf[2 * iz + 1] = jnp.where(
            walled, (0.25 * y[1]) * gy[32, pl.ds(iz * 16 + 8, 8), :], flux[2 * iz + 1]
        )

    drain(recv.at[6], rex)
    first, second = gas(*gather_sums(rex), sub, True)
    first, second = pltpu.roll(first, 1 - ip, 1), pltpu.roll(second, 1 - ip, 1)
    even = (lane & 7) == 2 - ip

    def packed(t, i):
        return jnp.where(even, spread(t[i : i + 1]), pltpu.roll(spread(t[i + 1 : i + 2]), 4, 1))

    quarter_x = 0.25 * xi_x
    mix, weight, ux, uy = [packed(first, 2 * i) for i in range(4)]
    uz, half = packed(second, 0), packed(second, 2)
    ey = [jnp.exp(-((y[h] - uy) * (y[h] - uy)) * half) for h in range(2)]
    dx = xi_x - ux
    for iz in range(8):
        dz = (iz - 3.5) - uz
        b = quarter_x * weight * jnp.exp(-(dz * dz + dx * dx) * half)
        for h in range(2):
            i = iz * 2 + h
            g = jnp.where(is_pos, ge[i], gh[i])
            hf[i] = (quarter_x * mix) * g + ey[h] * b

    last = lane == 127

    @pl.loop(0, N)
    def _(o):
        for i in range(16):
            at = pl.ds(i * 8, 8)
            for row in range(2):
                r = 2 * o + row
                fv[r, at, :] = fv[r, at, :] - jnp.where(
                    last, pltpu.roll(hf[i], 125 - 4 * r + ip, 1), 0.0
                )

    for i in range(16):
        at = pl.ds(i * 8, 8)
        fv[31, at, :] = fv[31, at, :] - wf[i]
    drain(send.at[3], rx)
    drain(send.at[4], ry)
    drain(send.at[5], r32)
    drain(send.at[6], rex)
    drain(hsend.at[0], warm)

    def y_update(i):
        o = owner(i)
        first, second = ay[o, 0:8, :], ay[o, 8:12, :]
        low = y_flux(first, second, 0, gy, 2 * o, xi_x)
        high = y_flux(first, second, 1, gy, 2 * o + 1, xi_x)
        rows = (above(2 * o), 2 * o, 2 * o + 1)
        for k in range(0, 16, 8):
            ats = [pl.ds(i * 8, 8) for i in range(k, k + 8)]
            old = [[fv[r, at, :] for at in ats] for r in rows]
            for i, at in enumerate(ats):
                fv[rows[0], at, :] = old[0][i] - low[k + i]
                fv[rows[1], at, :] = old[1][i] + (low[k + i] - high[k + i])
                fv[rows[2], at, :] = old[2][i] + high[k + i]

    def above(r):
        return jnp.where(r == 0, ROWS, r - 1)

    y_update(0)

    @pl.loop(1, N)
    def _(i):
        arrival(1, near(i), ay)
        y_update(i)

    def x_flux(i, slot):
        o = owner(i)
        first, second = ax[o, 0:8, :], ax[o, 8:12, :]
        for row in range(2):
            mix, ey, bz = factors(first, second, row, y, zed, xi_x)
            mix = quarter_x * mix
            bz = quarter_x * bz
            for iz in range(8):
                b = spread(bz[iz : iz + 1])
                for h in range(2):
                    at = pl.ds(iz * 16 + h * 8, 8)
                    fresh[slot, row, at, :] = mix * gx[2 * o + row, at, :] + ey[h] * b

    def x_rolls(slot):
        for row in range(2):
            for k in range(16):
                at = pl.ds(k * 8, 8)
                flux = fresh[slot, row, at, :]
                slots[slot, 0, row, at, :] = flux
                slots[slot, 1, row, at, :] = pltpu.roll(flux, 127, 1)

    def x_update(i, slot):
        o = owner(i)
        for row in range(2):
            r = 2 * o + row
            for k in range(16):
                at = pl.ds(k * 8, 8)
                beyond = jnp.where(last, 0.0, slots[slot, 1, row, at, :])
                plus[r, at, :] = fv[r, at, :] + (slots[slot, 0, row, at, :] - beyond)
            pltpu.make_async_copy(plus.at[r], out_hbm.at[:, r], out_sem.at[r]).start()

    x_flux(0, 0)
    arrival(2, near(1), ax)
    x_rolls(0)
    x_flux(1, 1)

    @pl.loop(1, 8)
    def _(k):
        i = 2 * k
        arrival(2, near(i), ax)
        x_rolls(1)
        x_flux(i, 0)
        x_update(i - 2, 0)
        arrival(2, near(i + 1), ax)
        x_rolls(0)
        x_flux(i + 1, 1)
        x_update(i - 1, 1)

    x_rolls(1)
    x_update(14, 0)
    x_update(15, 1)

    drain(hrecv.at[1], heat)
    piece = lax.broadcasted_iota(jnp.int32, (16, LANES), 0) + sp * 16
    piecef = piece.astype(F32)
    gained = jnp.zeros((16, LANES), F32)
    for k in range(N):
        t = heat[k]
        gained = gained + jnp.where(
            jnp.broadcast_to(t[1:2], (16, LANES)) == piecef,
            jnp.broadcast_to(t[0:1], (16, LANES)),
            0.0,
        )
    gained = jnp.sum(gained, axis=1, keepdims=True)
    own = jnp.broadcast_to(column(sp), (16, LANES))
    dev = own - 1.0
    before = column(lax.rem(sp + N - 1, N))[15:16] - 1.0
    after = column(lax.rem(sp + 1, N))[0:1] - 1.0
    before = jnp.broadcast_to(jnp.where(sp == 0, 0.0, 1.0) * before, (1, LANES))
    after = jnp.broadcast_to(jnp.where(sp == N - 1, 0.0, 1.0) * after, (1, LANES))
    dev_before = jnp.concatenate([before, dev[:-1]], axis=0)
    dev_after = jnp.concatenate([dev[1:], after], axis=0)
    new = own + 0.45 * (dev_before - 2.0 * dev + dev_after) + 0.025 * gained
    rev_ref[...] = jnp.sum(jnp.where(on_diag, new, 0.0), axis=0, keepdims=True)[:, 0:16]

    rev_copy = pltpu.make_async_copy(rev_ref, rev_hbm, out_sem.at[ROWS])
    rev_copy.start()
    drain(send.at[7], ax)
    drain(hsend.at[1], heat)

    drain(send.at[8], ay)
    rev_copy.wait()

    @pl.loop(0, ROWS)
    def _(r):
        pltpu.make_async_copy(plus.at[r], out_hbm.at[:, r], out_sem.at[r]).wait()


def hand_over(from_hbm, rev_from, to_hbm, rev_to, held, rev_held, sem):
    pieces = [(from_hbm.at[pl.ds(16 * i, 16)], held.at[i], to_hbm.at[pl.ds(16 * i, 16)]) for i in range(8)]
    pieces.append((rev_from, rev_held, rev_to))
    copies = [
        (pltpu.make_async_copy(a, b, sem.at[0, i]), pltpu.make_async_copy(b, c, sem.at[1, i]))
        for i, (a, b, c) in enumerate(pieces)
    ]
    for c, _d in copies:
        c.start()
    for c, d in copies:
        c.wait()
        d.start()
    for _c, d in copies:
        d.wait()


def per_device(particle_distribution, piece_warmth, exterior_piece_label):
    tile = functools.partial(pltpu.VMEM, dtype=F32)
    dma = pltpu.SemaphoreType.DMA
    hbm = pl.BlockSpec(memory_space=pltpu.HBM)
    one = tile((N, 8, LANES))
    two = tile((N, 12, LANES))
    flat = tile((8, LANES))
    shape = functools.partial(jax.ShapeDtypeStruct, dtype=F32)
    out, revised = pl.pallas_call(
        kernel,
        out_shape=(shape(particle_distribution.shape), shape((1, 16))),
        in_specs=[hbm] * 3,
        out_specs=(hbm, hbm),
        scratch_shapes=[
            tile((ROWS + 1, 128, LANES)), tile((ROWS + 1, 128, LANES)), two, one, tile((1, 16)),
            tile((ROWS + 4, 128, LANES)), tile((ROWS, 128, LANES)),
            tile((1, 16)), pltpu.VMEM((1, LANES), jnp.int32),
            one, one, two,
            one, one, two,
            one, one,
            flat, one,
            flat, one,
            flat, one,
            tile((N, 1, LANES)), one,
            one, one, one, one, one, one, tile((2, 3, 2, 128, LANES)), tile((2, 2, 128, LANES)),
            dma((ROWS + 2,)), dma((ROWS + 1,)),
            dma((9,)), dma((9,)), dma((3, N)), dma((4,)), dma((4,)),
        ],
        compiler_params=pltpu.CompilerParams(
            collective_id=0, has_side_effects=True, vmem_limit_bytes=62 * 1024 * 1000
        ),
    )(
        particle_distribution,
        piece_warmth.reshape(1, 16),
        exterior_piece_label.reshape(1, LANES),
    )
    out, revised = pl.pallas_call(
        hand_over,
        out_shape=(shape(particle_distribution.shape), shape((1, 16))),
        in_specs=[hbm] * 2,
        out_specs=(hbm, hbm),
        scratch_shapes=[tile((8, 16, ROWS, LANES)), tile((1, 16)), dma((2, 9))],
        compiler_params=pltpu.CompilerParams(vmem_limit_bytes=62 * 1024 * 1000),
    )(out, revised)
    return out, revised.reshape(16)


def solution(mesh):
    return jax.shard_map(
        per_device,
        mesh=mesh,
        in_specs=(P("vel", None, "space"), P("space"), P("space")),
        out_specs=(P("vel", None, "space"), P("space")),
        check_vma=False,
    )
```
